32 devices in a mesh: dp: 4 (over y, x), tensor: 8 (over z, core).
Axes of the slice: x: 2, y: 2, z: 4, core: 2. Of those that a mesh axis runs over, the one named last changes fastest.
Arguments:
- image: bfloat16 [8192, 2048], P(('dp', 'tensor')), may hold values from -6 to 6
- text: bfloat16 [4096, 4096], P('dp'), may hold values from -6 to 6
- cotangent: bfloat16 [8192, 2048], P(('dp', 'tensor')), may hold values from -6 to 6
- norm_gains: float32 [3, 2048], replicated, may hold values from 0.5 to 1.5
- norm_shifts: float32 [3, 2048], replicated, may hold values from -1.75 to 1.75
- w_self: bfloat16 [3, 2048, 2048], P(None, None, 'tensor'), may hold values from -1 to 1
- w_self_out: bfloat16 [2048, 2048], P('tensor'), may hold values from -0.5 to 0.5
- w_cross_q: bfloat16 [2048, 2048], P(None, 'tensor'), may hold values from -1 to 1
- w_cross_kv: bfloat16 [2, 2048, 2048], P(None, None, 'tensor'), may hold values from -0.125 to 0.125
- w_cross_out: bfloat16 [2048, 2048], P('tensor'), may hold values from -0.375 to 0.375
- w_text: bfloat16 [4096, 2048], P(None, 'tensor'), may hold values from -0.09375 to 0.09375
- w_up: bfloat16 [2048, 8192], P(None, 'tensor'), may hold values from -1 to 1
- w_down: bfloat16 [8192, 2048], P('tensor'), may hold values from -0.0625 to 0.0625
- segment_ids: int32 [8, 1024], P('dp'), may hold values from 0 to 3, never falling along the last dimension, each value on 1 to 384 neighbouring positions
- caption_lengths: int32 [32], P('dp'), may hold values from 32 to 128, as said below
Outputs:
- image_out: bfloat16 [8192, 2048], P(('dp', 'tensor'))
- image_grad: bfloat16 [8192, 2048], P(('dp', 'tensor'))
- text_grad: bfloat16 [4096, 4096], P(('dp', 'tensor'))
- gain_grad: float32 [3, 2048], replicated
- shift_grad: float32 [3, 2048], replicated
- self_grad: float32 [3, 2048, 2048], P(None, None, 'tensor')
- self_out_grad: float32 [2048, 2048], P('tensor')
- cross_q_grad: float32 [2048, 2048], P(None, 'tensor')
- cross_kv_grad: float32 [2, 2048, 2048], P(None, None, 'tensor')
- cross_out_grad: float32 [2048, 2048], P('tensor')
- text_w_grad: float32 [4096, 2048], P(None, 'tensor')
- up_grad: float32 [2048, 8192], P(None, 'tensor')
- down_grad: float32 [8192, 2048], P('tensor')
The draws below stay inside these ranges and needn't reach their ends.
Inputs may be any that keep to these rules, and one draw needn't show every extreme that they name: `segment_ids`: within a row the image number never falls and each of the 4 images has a token; some image has exactly 384 tokens. `caption_lengths`: A caption's live tokens fill the first slots of its 128; some caption is full and some has 32.
All inputs are finite; a program needn't handle non-finite values.
Results may differ from the reference program's by a relative error of at most 0.033.
Values may be sent and summed in bfloat16 or wider, within the bound.
A program may use at most 320 MiB of HBM per device.

```python
import math
import jax
import jax.numpy as jnp
import numpy as np
from jax import lax

D = 2048
H = 16
HD = 128
FF = 8192
TD = 4096
LEN = 1024
IMGS = 4
CAP = 128
ATT = 2048
ROWS = 8
TOKENS = 8192
CAPTIONS = 32
TEXT = 4096


def draw_caption_lengths(key, part):
    key = jax.random.fold_in(key, 7)
    first, second = jax.random.split(key)
    lengths = jax.random.randint(first, (CAPTIONS,), CAP // 4, CAP + 1)
    chosen = jax.random.randint(second, (), 0, CAPTIONS)
    places = jnp.arange(CAPTIONS)
    lengths = jnp.where(places == chosen, CAP, lengths)
    lengths = jnp.where(places == (chosen + 1) % CAPTIONS, CAP // 4, lengths)
    return lengths.astype(jnp.int32)


def column_weight(key, shape, fan_in):
    rough_key, common_key = jax.random.split(key)
    root_three = math.sqrt(3.0)
    rough = jax.random.uniform(rough_key, shape, jnp.float32, -1.0, 1.0) * root_three
    common_shape = shape[:-2] + (1, shape[-1])
    common = jax.random.uniform(common_key, common_shape, jnp.float32, -1.0, 1.0) * root_three
    return ((rough + 0.4 * common) * fan_in ** (-0.5)).astype(jnp.bfloat16)


def draw_w_self(key, part):
    key = jax.random.fold_in(key, 11)
    return column_weight(key, (3, D, ATT), D)


def draw_w_cross_q(key, part):
    key = jax.random.fold_in(key, 12)
    return column_weight(key, (D, ATT), D)


def draw_w_up(key, part):
    key = jax.random.fold_in(key, 13)
    return column_weight(key, (D, FF), D)


def levels(rng, dims, pieces, least, top_value):
    factor_of, own = 1.0, jax.random.fold_in(rng, 6)
    for position, parts in pieces:
        draws = jnp.exp(jax.random.uniform(jax.random.fold_in(own, position), (parts,), jnp.float32, least / len(pieces), top_value / len(pieces)))
        factor_of = factor_of * jnp.repeat(draws, dims[position] // parts).reshape([-1 if axis == position else 1 for axis in range(len(dims))])
    return factor_of


def split_up(count, total, bound, skew):
    loads = [(1 << 20) // math.isqrt(standing ** skew) + 1 for standing in range(2, count + 1)]
    surplus, holding = total - bound - (count - 1), [1] * (count - 1)
    while surplus > 0:
        candidates = [i for i in range(count - 1) if holding[i] < bound]
        whole, left = sum([loads[i] for i in candidates]), surplus
        for i in candidates:
            more = min(bound - holding[i], max(1, left * loads[i] // whole), surplus)
            holding[i] = holding[i] + more
            surplus = surplus - more
    return np.array([bound] + holding)


def ragged_sizes(own_key, amount, total, most, slope):
    if amount == 2:
        one = jax.random.randint(own_key, (), max(1, total - most), min(most, total - 1) + 1)
        return jnp.stack([one, total - one])
    tallies = jnp.asarray(split_up(amount, total, most, slope), jnp.int32)
    twos = (amount - 1) // 2
    giver, sink = tallies[1:1 + 2 * twos:2], tallies[2:2 + 2 * twos:2]
    margin = jnp.minimum(giver - 1, most - sink)
    passed = jax.random.randint(jax.random.fold_in(own_key, 1), (twos,), 0, 1 << 20) % (margin + 1)
    tallies = tallies.at[1:1 + 2 * twos:2].set(giver - passed).at[2:2 + 2 * twos:2].set(sink + passed)
    return tallies[jax.random.permutation(jax.random.fold_in(own_key, 2), amount)]


def bell_draw(stream_key, dims, deviation, bound, pieces=(), dtype=jnp.bfloat16):
    values = jax.random.normal(stream_key, dims, jnp.float32) * deviation
    if len(pieces) > 0:
        values = levels(stream_key, dims, pieces, -0.22, 0.18) * values
    return jnp.clip(values, min=-bound, max=bound).astype(dtype)


def setup_inputs(seed: int = 0) -> dict:
    splits = jax.random.split(jax.random.key(seed), 16)
    image = bell_draw(splits[0], (TOKENS, D), 1.0, 6.0, ((0, 32),))
    text = bell_draw(splits[1], (TEXT, TD), 1.0, 6.0, ((0, 4),))
    cotangent = bell_draw(splits[2], (TOKENS, D), 1.0, 6.0, ((0, 32),))
    norm_gains = jnp.clip(1.0 + 0.1 * jax.random.normal(splits[3], (3, D), jnp.float32), 0.5, 1.5)
    norm_shifts = bell_draw(splits[4], (3, D), 0.3, 1.75, (), jnp.float32)
    w_self = draw_w_self(jax.random.fold_in(splits[15], 71), 0)
    w_self_out = bell_draw(splits[6], (ATT, D), (ATT // 16) ** -0.5, 0.5, ((0, 8),))
    w_cross_q = draw_w_cross_q(jax.random.fold_in(splits[15], 71), 0)
    w_cross_kv = bell_draw(splits[8], (2, D, ATT), D ** -0.5, 0.125, ((2, 8),))
    w_cross_out = bell_draw(splits[9], (ATT, D), (ATT // 8) ** -0.5, 0.375, ((0, 8),))
    w_text = bell_draw(splits[10], (TD, D), TD ** -0.5, 0.09375, ((1, 8),))
    w_up = draw_w_up(jax.random.fold_in(splits[15], 71), 0)
    w_down = bell_draw(splits[12], (FF, D), FF ** -0.5, 0.0625, ((0, 8),))
    segment_ids = jax.vmap(lambda own: jnp.searchsorted(jnp.cumsum(ragged_sizes(own, IMGS, LEN, 3 * LEN // 8, 0)), jnp.arange(LEN), side="right"))(jax.random.split(splits[13], ROWS)).reshape((ROWS, LEN)).astype(jnp.int32)
    caption_lengths = draw_caption_lengths(jax.random.fold_in(splits[15], 71), 0)
    return {"image": image, "text": text, "cotangent": cotangent, "norm_gains": norm_gains, "norm_shifts": norm_shifts, "w_self": w_self, "w_self_out": w_self_out, "w_cross_q": w_cross_q, "w_cross_kv": w_cross_kv, "w_cross_out": w_cross_out, "w_text": w_text, "w_up": w_up, "w_down": w_down, "segment_ids": segment_ids, "caption_lengths": caption_lengths}


@jax.custom_vjp
def low(v):
    return lax.optimization_barrier(v.astype(jnp.bfloat16)).astype(jnp.float32)

@jax.custom_vjp
def low_back(v):
    return v

def low_keep(v):
    return (low(v), None)

def low_pass(kept, grad):
    return (grad,)

def back_keep(v):
    return (v, None)

def back_low(kept, grad):
    return (low(grad),)
low.defvjp(low_keep, low_pass)
low_back.defvjp(back_keep, back_low)
epsilon = 1e-05
masked_value = -1e+30

def product(left, right):
    return jnp.dot(left, right, precision=lax.Precision.HIGHEST, preferred_element_type=jnp.float32)

def layer_norm(value, gain, shift):
    mean = lax.optimization_barrier(jnp.mean(value, axis=-1, keepdims=True))
    centered = value - mean
    spread = lax.optimization_barrier(jnp.mean(centered * centered, axis=-1, keepdims=True))
    return centered * lax.rsqrt(spread + epsilon) * gain + shift

def attend(query, keys, values, allowed):
    scale = HD ** (-0.5)
    raw = low_back(jnp.einsum('qhe,khe->hqk', query, keys, precision=lax.Precision.HIGHEST))
    scores = jnp.where(allowed[None], raw * scale, masked_value)
    highest = lax.optimization_barrier(jnp.max(scores, axis=-1, keepdims=True))
    raised = jnp.exp(scores - highest)
    shares = raised / lax.optimization_barrier(jnp.sum(raised, axis=-1, keepdims=True))
    return jnp.einsum('hqk,khe->qhe', low(shares), values, precision=lax.Precision.HIGHEST)

def attend_rows(query, keys, values, allowed):
    block = jax.checkpoint(lambda packed: attend(packed[0], packed[1], packed[2], packed[3]))
    return lax.map(block, (query, keys, values, allowed))

def split_heads(flat):
    return flat.reshape(ROWS, -1, H, HD)

def merge_heads(split):
    return split.reshape(-1, ATT)

def layer(image, text, norm_gains, norm_shifts, w_self, w_self_out, w_cross_q, w_cross_kv, w_cross_out, w_text, w_up, w_down, same_image, cross_allowed):
    normed = low(layer_norm(image, norm_gains[0], norm_shifts[0]))
    triple = low_back(low(jnp.einsum('td,cde->cte', normed, w_self, precision=lax.Precision.HIGHEST)))
    mixed = attend_rows(split_heads(triple[0]), split_heads(triple[1]), split_heads(triple[2]), same_image)
    mixed = low_back(low(merge_heads(mixed)))
    stream_one = image + low_back(product(mixed, w_self_out))
    normed = low(layer_norm(stream_one, norm_gains[1], norm_shifts[1]))
    query = low_back(low(product(normed, w_cross_q)))
    projected = low_back(low(product(text, w_text)))
    pair = low_back(low(jnp.einsum('td,cde->cte', projected, w_cross_kv, precision=lax.Precision.HIGHEST)))
    mixed = attend_rows(split_heads(query), split_heads(pair[0]), split_heads(pair[1]), cross_allowed)
    mixed = low_back(low(merge_heads(mixed)))
    stream_two = stream_one + low_back(product(mixed, w_cross_out))
    normed = low(layer_norm(stream_two, norm_gains[2], norm_shifts[2]))
    hidden = low_back(product(normed, w_up))
    active = low(jax.nn.gelu(hidden, approximate=True))
    return stream_two + low_back(product(active, w_down))

def reference(image, text, cotangent, norm_gains, norm_shifts, w_self, w_self_out, w_cross_q, w_cross_kv, w_cross_out, w_text, w_up, w_down, segment_ids, caption_lengths):
    same_image = segment_ids[:, :, None] == segment_ids[:, None, :]
    slot = jnp.arange(IMGS * CAP).astype(jnp.int32)
    lengths = caption_lengths.reshape(ROWS, IMGS)
    live = (slot % CAP)[None, :] < jnp.repeat(lengths, CAP, axis=1)
    own_caption = segment_ids[:, :, None] == (slot // CAP)[None, None, :]
    cross_allowed = own_caption & live[:, None, :]
    floats = (image, text, norm_gains, norm_shifts, w_self, w_self_out, w_cross_q, w_cross_kv, w_cross_out, w_text, w_up, w_down)
    floats = tuple((value.astype(jnp.float32) for value in floats))

    def forward(*values):
        return layer(*values, same_image, cross_allowed)
    result, pull = jax.vjp(forward, *floats)
    grads = pull(cotangent.astype(jnp.float32))
    return (result.astype(jnp.bfloat16), grads[0].astype(jnp.bfloat16), grads[1].astype(jnp.bfloat16), grads[2], grads[3], grads[4], grads[5], grads[6], grads[7], grads[8], grads[9], grads[10], grads[11])
```

```python
import functools

import jax
import jax.numpy as jnp
from jax import lax
from jax.experimental import pallas as pl
from jax.experimental.pallas import tpu as pltpu
from jax.sharding import PartitionSpec as P

HD = 128
IMGS = 4
CAP = 128
SCALE = HD ** (-0.5)
MIB = 1024 * 1024

epsilon = 1e-05
masked_value = -1e30

TENSOR = "tensor"
DP = "dp"

F32 = jnp.float32
BF16 = jnp.bfloat16


def shares_of(q, k, allowed):
    raw = lax.dot_general(q, k, (((1,), (1,)), ((), ())), preferred_element_type=F32)
    scores = jnp.where(allowed, raw * SCALE, masked_value)
    highest = jnp.max(scores, axis=-1, keepdims=True)
    raised = jnp.exp(scores - highest)
    return raised * (1.0 / jnp.sum(raised, axis=-1, keepdims=True))


def attend_kernel(step, qid_ref, kid_ref, q_ref, k_ref, v_ref, o_ref):
    k = k_ref[...]
    v = v_ref[...]
    kid = kid_ref[...]
    for start in range(0, q_ref.shape[0], step):
        rows = pl.ds(start, step)
        shares = shares_of(q_ref[rows, :], k, qid_ref[rows, :] == kid)
        mixed = jnp.dot(shares.astype(BF16), v, preferred_element_type=F32)
        o_ref[rows, :] = mixed.astype(BF16)


def attend_back_kernel(step, qid_ref, kid_ref, q_ref, k_ref, v_ref, do_ref, dq_ref, dk_ref, dv_ref, dk_sum, dv_sum):
    k = k_ref[...]
    v = v_ref[...]
    kid = kid_ref[...]
    for start in range(0, q_ref.shape[0], step):
        rows = pl.ds(start, step)
        q = q_ref[rows, :]
        do = do_ref[rows, :]
        shares = shares_of(q, k, qid_ref[rows, :] == kid)
        dp = lax.dot_general(do, v, (((1,), (1,)), ((), ())), preferred_element_type=F32)
        inner = jnp.sum(dp * shares, axis=-1, keepdims=True)
        ds = (SCALE * (shares * (dp - inner))).astype(BF16)
        dq_ref[rows, :] = jnp.dot(ds, k, preferred_element_type=F32).astype(BF16)
        dk = lax.dot_general(ds, q, (((0,), (0,)), ((), ())), preferred_element_type=F32)
        dv = lax.dot_general(
            shares.astype(BF16), do, (((0,), (0,)), ((), ())), preferred_element_type=F32
        )
        if start == 0:
            dk_sum[...] = dk
            dv_sum[...] = dv
        else:
            dk_sum[...] += dk
            dv_sum[...] += dv
    dk_ref[...] = dk_sum[...].astype(BF16)
    dv_ref[...] = dv_sum[...].astype(BF16)


def head_spec(rows, which):
    if which is None:
        return pl.BlockSpec((rows, HD), lambda h: (0, h))
    return pl.BlockSpec((None, rows, HD), lambda h: (which, 0, h))


def whole_spec(shape):
    return pl.BlockSpec(shape, lambda h: (0, 0))


def attend(qid, kid, query, keys, values):
    (qa, qp), (ka, kp), (va, vp) = query, keys, values
    tokens, width = qa.shape[-2:]
    slots = ka.shape[-2]
    heads = width // HD
    return pl.pallas_call(
        functools.partial(attend_kernel, 256),
        grid=(heads,),
        in_specs=[
            whole_spec(qid.shape),
            whole_spec(kid.shape),
            head_spec(tokens, qp),
            head_spec(slots, kp),
            head_spec(slots, vp),
        ],
        out_specs=head_spec(tokens, None),
        out_shape=jax.ShapeDtypeStruct((tokens, width), BF16),
        compiler_params=pltpu.CompilerParams(vmem_limit_bytes=48 * MIB),
        cost_estimate=pl.CostEstimate(
            flops=4 * tokens * slots * width,
            bytes_accessed=2 * width * (2 * tokens + 2 * slots),
            transcendentals=tokens * slots * heads,
        ),
        name="attend",
    )(qid, kid, qa, ka, va)


def attend_back(qid, kid, query, keys, values, do):
    (qa, qp), (ka, kp), (va, vp) = query, keys, values
    tokens, width = qa.shape[-2:]
    slots = ka.shape[-2]
    heads = width // HD
    return pl.pallas_call(
        functools.partial(attend_back_kernel, 256),
        grid=(heads,),
        in_specs=[
            whole_spec(qid.shape),
            whole_spec(kid.shape),
            head_spec(tokens, qp),
            head_spec(slots, kp),
            head_spec(slots, vp),
            head_spec(tokens, None),
        ],
        out_specs=[head_spec(tokens, None), head_spec(slots, None), head_spec(slots, None)],
        out_shape=[
            jax.ShapeDtypeStruct((tokens, width), BF16),
            jax.ShapeDtypeStruct((slots, width), BF16),
            jax.ShapeDtypeStruct((slots, width), BF16),
        ],
        scratch_shapes=[pltpu.VMEM((slots, HD), F32), pltpu.VMEM((slots, HD), F32)],
        compiler_params=pltpu.CompilerParams(vmem_limit_bytes=48 * MIB),
        cost_estimate=pl.CostEstimate(
            flops=10 * tokens * slots * width,
            bytes_accessed=2 * width * (3 * tokens + 4 * slots),
            transcendentals=tokens * slots * heads,
        ),
        name="attend_back",
    )(qid, kid, qa, ka, va, do)


def dot(left, right):
    return jnp.dot(left, right, preferred_element_type=F32)


def dot_t(left, right):
    return lax.dot_general(left, right, (((0,), (0,)), ((), ())), preferred_element_type=F32)


def dot_r(left, right):
    return lax.dot_general(left, right, (((1,), (1,)), ((), ())), preferred_element_type=F32)


def planes_of(left, right):
    return jnp.einsum("td,cde->cte", left, right, preferred_element_type=F32).astype(BF16)


def planes_grad(left, right):
    return jnp.einsum("td,cta->cda", left, right, preferred_element_type=F32).astype(BF16)


def planes_back(left, right):
    return jnp.einsum("cta,cda->td", left, right, preferred_element_type=F32).astype(BF16)


def norm_parts(value):
    mean = jnp.mean(value, axis=-1, keepdims=True)
    centered = value - mean
    spread = jnp.mean(centered * centered, axis=-1, keepdims=True)
    rate = lax.rsqrt(spread + epsilon)
    return centered * rate, rate


def gelu_parts(h):
    c = 0.7978845608028654
    inner = c * (h + 0.044715 * h * h * h)
    th = jnp.tanh(inner)
    half = 0.5 * (1.0 + th)
    slope = half + 0.5 * h * (1.0 - th * th) * (c * (1.0 + 3 * 0.044715 * h * h))
    return h * half, slope


def partner(index, bit):
    return index + bit - 2 * bit * ((index // bit) % 2)


def peer(index, mask):
    bit = 1
    while bit <= mask:
        if mask & bit:
            index = partner(index, bit)
        bit *= 2
    return index


def low_bit(value):
    return value & -value


def high_bit(value):
    return 1 << (value.bit_length() - 1)


def level_of(value):
    return sum((value >> i) & 1 for i in range(value.bit_length()))


def bits_of(size):
    return tuple(1 << i for i in range(size.bit_length() - 1))


def remote(src, dst, send_sem, recv_sem, axis, index):
    copy = pltpu.make_async_remote_copy(
        src_ref=src,
        dst_ref=dst,
        send_sem=send_sem,
        recv_sem=recv_sem,
        device_id={axis: index},
        device_id_type=pl.DeviceIdType.MESH,
    )
    copy.start()
    return copy


def local_copy(src, dst, sem):
    copy = pltpu.make_async_copy(src, dst, sem)
    copy.start()
    return copy


VMEM = pl.BlockSpec(memory_space=pltpu.VMEM)
HBM = pl.BlockSpec(memory_space=pl.ANY)
DMA = pltpu.SemaphoreType.DMA


class Flow:
    def __init__(self, partners):
        self.partners = partners
        self.ins, self.outs, self.scratch = [], [], []
        self.steps = None

    def take(self, array, spec=HBM):
        self.ins.append((array, spec))
        return (0, len(self.ins) - 1)

    def give(self, shape, dtype, spec=HBM):
        self.outs.append((jax.ShapeDtypeStruct(shape, dtype), spec))
        return (1, len(self.outs) - 1)

    def hold(self, kind):
        self.scratch.append((kind, None))
        return (2, len(self.scratch) - 1)

    def vmem(self, *shape, dtype=BF16):
        return self.hold(pltpu.VMEM(shape, dtype))

    def sems(self, *shape):
        return self.hold(DMA(shape))


def flows_kernel(flows, *refs):
    refs = list(refs)
    tables = [{} for unused in flows]
    for part in range(3):
        for flow, table in zip(flows, tables):
            for i in range(len((flow.ins, flow.outs, flow.scratch)[part])):
                table[part, i] = refs.pop(0)
    partners = []
    for flow in flows:
        partners += [entry for entry in flow.partners if entry not in partners]
    barrier = pltpu.get_barrier_semaphore()
    for axis, bit in partners:
        pl.semaphore_signal(
            barrier,
            inc=1,
            device_id={axis: partner(lax.axis_index(axis), bit)},
            device_id_type=pl.DeviceIdType.MESH,
        )
    pl.semaphore_wait(barrier, len(partners))
    running = [[0.0, flow.steps(table)] for flow, table in zip(flows, tables)]
    while running:
        entry = min(running, key=lambda e: e[0])
        moment = next(entry[1], None)
        if moment is None:
            running.remove(entry)
        else:
            entry[0] = moment


def run_flows(cid, name, micros, *flows):
    ins, outs, scratch = [
        [entry for flow in flows for entry in part(flow)]
        for part in (lambda f: f.ins, lambda f: f.outs, lambda f: f.scratch)
    ]
    results = pl.pallas_call(
        functools.partial(flows_kernel, flows),
        in_specs=[entry[1] for entry in ins],
        out_specs=[entry[1] for entry in outs],
        out_shape=[entry[0] for entry in outs],
        scratch_shapes=[entry[0] for entry in scratch],
        compiler_params=pltpu.CompilerParams(
            collective_id=cid, has_side_effects=True, vmem_limit_bytes=58 * MIB
        ),
        cost_estimate=pl.CostEstimate(
            flops=0, bytes_accessed=int(micros * 3.3e6), transcendentals=0
        ),
        name=name,
    )(*[entry[0] for entry in ins])
    results = list(results)
    return [tuple(results.pop(0) for unused in flow.outs) for flow in flows]


class Sum:
    def __init__(self, flow, size, chunks, high, wide):
        self.size, self.chunks = size, chunks
        self.held = flow.vmem(size // 2, high, wide)
        self.came = flow.vmem(size - 1, high, wide)
        self.load = flow.sems(size // 2, chunks)
        self.sent = flow.sems(size, chunks)
        self.got = flow.sems(size, chunks)

    def steps(self, r, view, rows, finish, clock):
        bits = bits_of(self.size)
        chunks = self.chunks
        index = lax.axis_index(TENSOR)
        held, came = r[self.held], r[self.came]
        firsts = sorted(range(0, self.size, 2), reverse=True)
        sent, loads = {}, {}

        def send(src, block, chunk, bit):
            sent[block, chunk] = remote(
                src,
                came.at[block - 1, rows(chunk)],
                r[self.sent].at[block, chunk],
                r[self.got].at[block, chunk],
                TENSOR,
                partner(index, bit),
            )

        def summed(block, chunk):
            loads[block, chunk].wait()
            total = held[block // 2, rows(chunk)].astype(F32)
            for bit in bits:
                if block == 0 or bit < low_bit(block):
                    sent[block + bit, chunk].wait_recv()
                    total = total + came[block + bit - 1, rows(chunk)].astype(F32)
            return total

        for block in firsts:
            for chunk in range(chunks):
                send(view(block + 1, chunk), block + 1, chunk, 1)
                loads[block, chunk] = local_copy(
                    view(block, chunk),
                    held.at[block // 2, rows(chunk)],
                    r[self.load].at[block // 2, chunk],
                )
        start, middle, pace, last = clock
        yield start
        for block in firsts:
            if block:
                for chunk in range(chunks):
                    if low_bit(block) > 2:
                        yield middle + chunk * pace
                    held[block // 2, rows(chunk)] = summed(block, chunk).astype(BF16)
                    send(held.at[block // 2, rows(chunk)], block, chunk, low_bit(block))
        for chunk in range(chunks):
            yield last + chunk * pace
            finish(chunk, summed(0, chunk))
        for copy in sent.values():
            copy.wait_send()


def norm_back_parts(value, gain, gradient):
    xh, rate = norm_parts(value)
    mg = gradient * gain
    back = rate * (
        mg - jnp.mean(mg, axis=-1, keepdims=True) - xh * jnp.mean(mg * xh, axis=-1, keepdims=True)
    )
    return back, jnp.sum(gradient * xh, axis=0, keepdims=True), jnp.sum(gradient, axis=0, keepdims=True)


def stream_flow(
    value=None,
    gain=None,
    shift=None,
    terms=None,
    above=None,
    rs=1,
    ag=1,
    keep=True,
    late=None,
    everyone=(),
    clock=(5, 30, 6, 60),
    gather_clock=(30, 6),
):
    if value is None:
        tokens, model = terms.shape[0] // rs, terms.shape[1]
    else:
        tokens, model = value.shape
    ag_bits = bits_of(ag)
    chunks = 4 if tokens % 64 == 0 else 1
    part = tokens // chunks
    flow = Flow([(TENSOR, bit) for bit in bits_of(max(rs, ag))] + list(everyone))
    if value is not None:
        value_key = flow.take(value, VMEM)
        gain_key = flow.take(gain[None], VMEM)
    if shift is not None:
        shift_key = flow.take(shift[None], VMEM)
    if above is not None:
        above_key = flow.take(above, VMEM)
        gain_sum = flow.give((1, model), F32, VMEM)
        shift_sum = flow.give((1, model), F32, VMEM)
    if rs > 1:
        terms_key = flow.take(terms)
        total_of = Sum(flow, rs, chunks, tokens, model)
    if keep:
        stream_key = flow.give((tokens, model), F32, VMEM)
    result_key = flow.give((ag * tokens, model), BF16, HBM if ag > 1 else VMEM)
    if ag > 1:
        own_key = flow.vmem(tokens, model)
        keep_sem = flow.sems(chunks)
        ag_send = flow.sems(ag, chunks)
        ag_recv = flow.sems(ag, chunks)
    if late is not None:
        late_key = flow.take(late, VMEM)
        all_key = flow.give((8, model), F32, VMEM)
        totals_key = flow.vmem(len(everyone) + 1, 8, model, dtype=F32)
        others_key = flow.vmem(len(everyone), 8, model, dtype=F32)
        totals_send = flow.sems(len(everyone))
        totals_recv = flow.sems(len(everyone))

    def rows(chunk):
        return pl.ds(chunk * part, part)

    def steps(r):
        t = lax.axis_index(TENSOR)

        def at(block, group, chunk):
            start = (peer(t, block) % group) * tokens + chunk * part
            return pl.ds(pl.multiple_of(start, 16), part)

        sent, keeps = {}, []

        def send(src, dst, block, chunk, bit):
            sent[block, chunk] = remote(
                src,
                dst,
                r[ag_send].at[block, chunk],
                r[ag_recv].at[block, chunk],
                TENSOR,
                partner(t, bit),
            )

        def finish(chunk, total):
            here = rows(chunk)
            if value is None:
                r[result_key][here, :] = total.astype(BF16)
                return
            stream = r[value_key][here, :].astype(F32)
            if above is None:
                if total is not None:
                    stream = stream + total
                    r[stream_key][here, :] = stream
                xh, unused = norm_parts(stream)
                result = (xh * r[gain_key][...] + r[shift_key][...]).astype(BF16)
            else:
                back, gains, shifts = norm_back_parts(stream, r[gain_key][...], total)
                if chunk == 0:
                    r[gain_sum][...] = gains
                    r[shift_sum][...] = shifts
                else:
                    r[gain_sum][...] += gains
                    r[shift_sum][...] += shifts
                gradient = r[above_key][here, :].astype(F32) + back
                if keep:
                    r[stream_key][here, :] = gradient
                result = gradient.astype(BF16)
            if ag == 1:
                r[result_key][here, :] = result
                return
            r[own_key][here, :] = result
            place = r[result_key].at[at(0, ag, chunk)]
            keeps.append(local_copy(r[own_key].at[here], place, r[keep_sem].at[chunk]))
            for bit in reversed(ag_bits):
                send(r[own_key].at[here], place, bit, chunk, bit)

        if rs > 1:
            yield from total_of.steps(
                r,
                lambda block, chunk: r[terms_key].at[at(block, rs, chunk)],
                rows,
                finish,
                clock,
            )
        else:
            for chunk in range(chunks):
                finish(chunk, None)
        if late is not None:
            count = late.shape[0]
            totals, others = r[totals_key], r[others_key]
            totals[0, :count] = r[late_key][...]
            totals[0, count : count + 1] = r[gain_sum][...]
            totals[0, count + 1 : count + 2] = r[shift_sum][...]
            totals[0, count + 2 :] = jnp.zeros_like(totals[0, count + 2 :])
            for i, (axis, bit) in enumerate(everyone):
                copy = remote(
                    totals.at[i],
                    others.at[i],
                    r[totals_send].at[i],
                    r[totals_recv].at[i],
                    axis,
                    partner(lax.axis_index(axis), bit),
                )
                yield clock[-1] + 40 + 15 * i
                copy.wait()
                totals[i + 1] = totals[i] + others[i]
            r[all_key][...] = totals[len(everyone)]
        first, pace = gather_clock
        for i, block in enumerate(sorted(range(2, ag, 2), key=lambda b: (level_of(b), low_bit(b)))):
            for chunk in range(chunks):
                yield first + (i * chunks + chunk) * pace
                sent[block, chunk].wait_recv()
                for bit in reversed(ag_bits):
                    if bit < low_bit(block):
                        place = r[result_key].at[at(block, ag, chunk)]
                        send(place, place, block + bit, chunk, bit)
        for (block, chunk), copy in sent.items():
            copy.wait_send()
            if block % 2:
                copy.wait_recv()
        for copy in keeps:
            copy.wait()

    flow.steps = steps
    return flow


def spread_on(side, block, bit):
    if block == 0:
        return True
    return bit < low_bit(block) if side == 0 else bit > high_bit(block)


def fetch_flow(weights, half, n_dp, window=3, clock=(8, 6.5)):
    dp_bits = bits_of(n_dp)
    units = [
        (which, plane, side)
        for which, (by_rows, weight) in enumerate(weights)
        for plane in range(weight.shape[0])
        for side in range(2)
    ]
    flow = Flow([(TENSOR, half)] + [(DP, bit) for bit in dp_bits])
    sources, targets, owns = [], [], []
    for by_rows, weight in weights:
        planes, high, wide = weight.shape
        sources.append(flow.take(weight))
        both = (planes, 2 * high, wide) if by_rows else (planes, high, 2 * wide)
        targets.append(flow.give(both, BF16))
        owns.append(flow.vmem(*weight.shape))
    sends = flow.sems(len(units), n_dp)
    recvs = flow.sems(len(units), n_dp)
    takes = flow.sems(len(weights))
    keep_sems = flow.sems(len(weights))

    def steps(r):
        t = lax.axis_index(TENSOR)
        d = lax.axis_index(DP)
        copies, keeps = {}, []

        def places(unit, block):
            which, plane, side = unit
            by_rows, weight = weights[which]
            source, target = r[sources[which]], r[targets[which]]
            high, wide = weight.shape[1:]
            size = (wide if by_rows else high) // n_dp // 2
            start = (peer(d, block) * 2 + side) * size
            if by_rows:
                columns = pl.ds(pl.multiple_of(start, 128), size)
                return source.at[plane, :, columns], target.at[plane, pl.ds(high, high), columns]
            rows = pl.ds(pl.multiple_of(start, 16), size)
            return source.at[plane, rows], target.at[plane, rows, pl.ds(wide, wide)]

        def send(src, dst, unit, block, axis, index):
            copies[unit, block] = remote(
                src, dst, r[sends].at[unit, block], r[recvs].at[unit, block], axis, index
            )

        def begin(unit):
            if unit < len(units):
                src, dst = places(units[unit], 0)
                send(src, dst, unit, 0, TENSOR, partner(t, half))

        def forward(unit, block):
            copies[unit, block].wait_recv()
            place = places(units[unit], block)[1]
            for bit in dp_bits:
                if spread_on(units[unit][2], block, bit):
                    send(place, place, unit, block + bit, DP, partner(d, bit))

        for unit in range(window):
            begin(unit)
        for which in range(len(weights)):
            keeps.append(local_copy(r[sources[which]], r[owns[which]], r[takes].at[which]))
        yield clock[0]
        for which, (by_rows, weight) in enumerate(weights):
            high, wide = weight.shape[1:]
            target = r[targets[which]]
            target = target.at[:, pl.ds(0, high)] if by_rows else target.at[:, :, pl.ds(0, wide)]
            keeps[which].wait()
            keeps[which] = local_copy(r[owns[which]], target, r[keep_sems].at[which])
        for step in range(len(units) + len(dp_bits) - 1):
            if step < len(units):
                forward(step, 0)
                begin(step + window)
            for level in range(1, len(dp_bits)):
                if 0 <= step - level < len(units):
                    for block in range(1, n_dp):
                        if level_of(block) == level:
                            forward(step - level, block)
            yield clock[0] + (step + 1) * clock[1]
        for unit in range(len(units)):
            copies[unit, n_dp - 1].wait_recv()
        for copy in copies.values():
            copy.wait_send()
        for copy in keeps:
            copy.wait()

    flow.steps = steps
    return flow


def text_flow(text, half, n, clock=(20, 12)):
    high, wide = text.shape[0] // (n // half), text.shape[1]
    flow = Flow([(TENSOR, bit) for bit in bits_of(n)])
    text_key = flow.take(text)
    result_key = flow.give((high, wide * n), BF16)
    own_key = flow.vmem(high, wide)
    sends, recvs, keeps = flow.sems(n), flow.sems(n), flow.sems(2)

    def steps(r):
        t = lax.axis_index(TENSOR)
        row = t // half
        copies = {}

        def rows(which):
            return r[text_key].at[pl.ds(pl.multiple_of(which * high, 16), high)]

        def columns(block):
            return r[result_key].at[:, pl.ds(pl.multiple_of(peer(t, block) * wide, 128), wide)]

        def send(src, dst, block, bit):
            copies[block] = remote(
                src, dst, r[sends].at[block], r[recvs].at[block], TENSOR, partner(t, bit)
            )

        for bit in reversed(bits_of(n)):
            send(rows(1 - row if bit == half else row), columns(0), bit, bit)
        keep = local_copy(rows(row), r[own_key], r[keeps].at[0])
        yield clock[0]
        keep.wait()
        keep = local_copy(r[own_key], columns(0), r[keeps].at[1])
        for i, block in enumerate(sorted(range(1, n), key=lambda b: (level_of(b), low_bit(b)))):
            copies[block].wait_recv()
            for bit in reversed(bits_of(n)):
                if bit < low_bit(block):
                    send(columns(block), columns(block), block + bit, bit)
            yield clock[0] + i * clock[1]
        for copy in copies.values():
            copy.wait_send()
        keep.wait()

    flow.steps = steps
    return flow


def text_back_flow(terms, half, n, clocks=((8, 30, 6, 30), (9, 30, 6, 35), 45)):
    high, wide = terms.shape[0], terms.shape[1] // n
    flow = Flow([(TENSOR, bit) for bit in bits_of(n)])
    terms_key = flow.take(terms)
    result_key = flow.give((high * (n // half), wide), BF16)
    sums = [Sum(flow, half, 1, high, wide) for unused in range(2)]
    owns = [flow.vmem(high, wide) for unused in range(2)]
    sems = flow.sems(3)

    def steps(r):
        t = lax.axis_index(TENSOR)
        row = t // half
        last = []

        def view(far):
            def place(block, chunk):
                column = peer(t, block + far) * wide
                return r[terms_key].at[:, pl.ds(pl.multiple_of(column, 128), wide)]

            return place

        def target():
            return r[result_key].at[pl.ds(pl.multiple_of(row * high, 16), high)]

        def finish_far(chunk, total):
            r[owns[0]][...] = total.astype(BF16)
            last.append(
                remote(
                    r[owns[0]],
                    target(),
                    r[sems].at[0],
                    r[sems].at[1],
                    TENSOR,
                    partner(t, half),
                )
            )

        def finish_near(chunk, total):
            r[owns[1]][...] = total.astype(BF16)
            last.append(local_copy(r[owns[1]], target(), r[sems].at[2]))

        def rows(chunk):
            return pl.ds(0, high)

        parts = [
            [0, sums[0].steps(r, view(half), rows, finish_far, clocks[0])],
            [0, sums[1].steps(r, view(0), rows, finish_near, clocks[1])],
        ]
        while parts:
            entry = min(parts, key=lambda e: e[0])
            if entry[0]:
                yield entry[0]
            moment = next(entry[1], None)
            if moment is None:
                parts.remove(entry)
            else:
                entry[0] = moment
        yield clocks[2]
        for copy in last:
            copy.wait()

    flow.steps = steps
    return flow


def grads_flow(grads, n_dp, half=0, summing=True, window=4, clock=(10, 20)):
    high, whole = grads[0].shape[1:]
    high = high if summing else high * n_dp
    wide = whole // 2 if half else whole
    size = high // n_dp // 2
    dp_bits = bits_of(n_dp)
    units = [
        (which, plane, side)
        for which, grad in enumerate(grads)
        for plane in range(grad.shape[0])
        for side in range(2)
    ]
    count = len(units)
    depth = len(dp_bits)
    slots = n_dp // 2 if summing else 1
    flow = Flow([(DP, bit) for bit in dp_bits] + ([(TENSOR, half)] if half else []))
    sources = [flow.take(grad) for grad in grads]
    targets = [flow.give((grad.shape[0], high, wide), BF16) for grad in grads]
    held = flow.vmem(count, slots, size, whole if summing else wide)
    load_sems = flow.sems(count, slots)
    if summing:
        came = flow.vmem(count, n_dp - 1, size, whole)
        sum_send, sum_recv = flow.sems(count, n_dp), flow.sems(count, n_dp)
    if half:
        given = flow.vmem(count, size, wide)
        mid_send, mid_recv = flow.sems(count), flow.sems(count)
        if summing:
            mine = flow.vmem(count, size, wide, dtype=F32)
            theirs = flow.vmem(count, size, wide)
    final = flow.vmem(count, size, wide)
    ag_send, ag_recv = flow.sems(count, n_dp), flow.sems(count, n_dp)
    keep_sems = flow.sems(count)

    def order(side):
        return dp_bits if side == 0 else tuple(reversed(dp_bits))

    def stage(side, block):
        return min(i for i, bit in enumerate(order(side)) if block & bit)

    def slot(side, block):
        return [b for b in range(n_dp) if b == 0 or stage(side, b) > 0].index(block)

    def steps(r):
        d = lax.axis_index(DP)
        sums, loads, mids, spreads, keeps = {}, {}, {}, {}, {}

        def region(keys, unit, block, piece=False):
            which, plane, side = units[unit]
            start = side * size if piece else (peer(d, block) * 2 + side) * size
            return r[keys[which]].at[plane, pl.ds(pl.multiple_of(start, 16), size)]

        def swap(src, unit):
            mids[unit] = remote(
                src,
                r[given].at[unit],
                r[mid_send].at[unit],
                r[mid_recv].at[unit],
                TENSOR,
                partner(lax.axis_index(TENSOR), half),
            )

        def send(src, unit, block):
            side = units[unit][2]
            sums[unit, block] = remote(
                src,
                r[came].at[unit, block - 1],
                r[sum_send].at[unit, block],
                r[sum_recv].at[unit, block],
                DP,
                partner(d, order(side)[stage(side, block)]),
            )

        def summed(unit, block):
            side = units[unit][2]
            loads[unit, block].wait()
            total = r[held][unit, slot(side, block)].astype(F32)
            for i, bit in enumerate(order(side)):
                if summing and (block == 0 or i < stage(side, block)):
                    sums[unit, block + bit].wait_recv()
                    total = total + r[came][unit, block + bit - 1].astype(F32)
            return total

        def begin(unit):
            if unit >= count:
                return
            side = units[unit][2]
            if not summing:
                source = region(sources, unit, 0, True)
                swap(source.at[:, pl.ds(wide, wide)], unit)
                loads[unit, 0] = local_copy(
                    source.at[:, pl.ds(0, wide)], r[held].at[unit, 0], r[load_sems].at[unit, 0]
                )
                return
            for block in range(n_dp):
                source = region(sources, unit, block)
                if block and stage(side, block) == 0:
                    send(source, unit, block)
                else:
                    place = slot(side, block)
                    loads[unit, block] = local_copy(
                        source, r[held].at[unit, place], r[load_sems].at[unit, place]
                    )

        def middle(unit, level):
            side = units[unit][2]
            for block in range(1, n_dp):
                if stage(side, block) == level:
                    r[held][unit, slot(side, block)] = summed(unit, block).astype(BF16)
                    send(r[held].at[unit, slot(side, block)], unit, block)

        def cross(unit):
            if half and summing:
                total = summed(unit, 0)
                r[mine][unit] = total[:, :wide]
                r[theirs][unit] = total[:, wide:].astype(BF16)
                swap(r[theirs].at[unit], unit)

        def spread(unit, block, src, dst):
            for bit in dp_bits:
                if spread_on(units[unit][2], block, bit):
                    spreads[unit, block + bit] = remote(
                        src,
                        dst,
                        r[ag_send].at[unit, block + bit],
                        r[ag_recv].at[unit, block + bit],
                        DP,
                        partner(d, bit),
                    )

        def settle(unit):
            total = r[mine][unit] if half and summing else summed(unit, 0)
            if half:
                mids[unit].wait_recv()
                total = total + r[given][unit].astype(F32)
            r[final][unit] = total.astype(BF16)
            place = region(targets, unit, 0)
            keeps[unit] = local_copy(r[final].at[unit], place, r[keep_sems].at[unit])
            spread(unit, 0, r[final].at[unit], place)

        def onward(unit, level):
            for block in range(1, n_dp):
                if level_of(block) == level:
                    spreads[unit, block].wait_recv()
                    place = region(targets, unit, block)
                    spread(unit, block, place, place)

        for unit in range(window):
            begin(unit)
        first = depth if summing else 0
        for step in range(count + first + depth):
            yield clock[0] + step * clock[1]

            def turn(lag, action, *more):
                if 0 <= step - lag < count:
                    action(step - lag, *more)

            for level in range(depth - 1, 0, -1):
                turn(first + level, onward, level)
            turn(first, settle)
            turn(max(first - 1, 0), cross)
            if summing:
                for level in range(depth - 1, 0, -1):
                    turn(level - 1, middle, level)
            begin(step + window)
        for unit in range(count):
            spreads[unit, n_dp - 1].wait_recv()
        for copy in [*sums.values(), *mids.values(), *spreads.values()]:
            copy.wait_send()
        for copy in keeps.values():
            copy.wait()

    flow.steps = steps
    return flow


def pass_flow(value):
    flow = Flow([])
    value_key = flow.take(value)
    result_key = flow.give(value.shape, value.dtype)
    held = flow.vmem(*value.shape)
    sems = flow.sems(2)

    def steps(r):
        copy = local_copy(r[value_key], r[held], r[sems].at[0])
        yield 8
        copy.wait()
        copy = local_copy(r[held], r[result_key], r[sems].at[1])
        yield 30
        copy.wait()

    flow.steps = steps
    return flow


def nothing(*refs):
    pass


def after(value, *before):
    return pl.pallas_call(
        nothing,
        in_specs=[HBM] * (1 + len(before)),
        out_specs=HBM,
        out_shape=jax.ShapeDtypeStruct(value.shape, value.dtype),
        input_output_aliases={0: 0},
    )(value, *before)


def local(
    image,
    text,
    cotangent,
    norm_gains,
    norm_shifts,
    w_self,
    w_self_out,
    w_cross_q,
    w_cross_kv,
    w_cross_out,
    w_text,
    w_up,
    w_down,
    segment_ids,
    caption_lengths,
):
    rows_here = segment_ids.shape[0]
    n_tensor = lax.axis_size(TENSOR)
    n_dp = lax.axis_size(DP)
    half = n_tensor // rows_here
    row = lax.axis_index(TENSOR) // half
    width = w_self.shape[2]
    slots = IMGS * CAP

    seg = lax.dynamic_index_in_dim(segment_ids, row, 0, keepdims=False)
    seg_col = seg[:, None]
    seg_row = seg[None, :]
    lengths = lax.dynamic_index_in_dim(caption_lengths.reshape(rows_here, IMGS), row, 0, keepdims=False)
    slot = jnp.arange(slots, dtype=jnp.int32)
    live = (slot % CAP) < jnp.repeat(lengths, CAP)
    slot_row = jnp.where(live, slot // CAP, -1)[None, :]

    (w_self2, w_self_out2), (n1,), (later,) = run_flows(
        0,
        "start",
        60,
        fetch_flow(((False, w_self), (True, w_self_out[None])), half, n_dp),
        stream_flow(
            image, norm_gains[0], norm_shifts[0], ag=half, keep=False, gather_clock=(12, 11)
        ),
        pass_flow(cotangent),
    )
    w_self_out2 = w_self_out2[0]
    triple = planes_of(n1, w_self2)
    o1 = attend(seg_col, seg_row, (triple, 0), (triple, 1), (triple, 2))
    p1 = dot(o1, w_self_out2).astype(BF16)
    e3 = lax.all_gather(later, TENSOR, axis=0, tiled=True)
    text_columns = dot(text, w_text).astype(BF16)
    (x1, n2), (w_kv2, w_cross_q2, w_cross_out2), (projected,) = run_flows(
        1,
        "self_sum",
        100,
        stream_flow(
            image,
            norm_gains[1],
            norm_shifts[1],
            terms=p1,
            rs=half,
            ag=half,
            clock=(5, 0, 10, 18),
            gather_clock=(60, 10),
        ),
        fetch_flow(
            ((False, w_cross_kv), (False, w_cross_q[None]), (True, w_cross_out[None])),
            half,
            n_dp,
            clock=(20, 8),
        ),
        text_flow(text_columns, half, n_tensor),
    )
    w_cross_q2, w_cross_out2 = w_cross_q2[0], w_cross_out2[0]

    pair = planes_of(projected, w_kv2)
    q2 = dot(n2, w_cross_q2).astype(BF16)
    o2 = attend(seg_col, slot_row, (q2, None), (pair, 0), (pair, 1))
    p2 = dot(o2, w_cross_out2).astype(BF16)
    ((x2, n3),) = run_flows(
        2,
        "cross_sum",
        100,
        stream_flow(x1, norm_gains[2], norm_shifts[2], terms=p2, rs=half, ag=n_tensor),
    )

    h = dot(n3, w_up)
    act, slope = gelu_parts(h)
    act = act.astype(BF16)
    slope = slope.astype(BF16)
    down_grad = dot_t(act, e3).astype(BF16)
    dh = (dot_r(e3, w_down) * slope.astype(F32)).astype(BF16)
    up_grad = dot_t(n3, dh).astype(BF16)
    sums = lax.psum((down_grad, up_grad), DP)
    p3 = after(dot_r(dh, w_up).astype(BF16), down_grad, up_grad)
    ((gain_two, shift_two, g2, e2),) = run_flows(
        3,
        "up_sum",
        100,
        stream_flow(
            x2, norm_gains[2], terms=p3, above=cotangent, rs=n_tensor, ag=half, clock=(8, 30, 6, 60)
        ),
    )

    do2 = dot_r(e2, w_cross_out2).astype(BF16)
    dq2, dk2, dv2 = attend_back(seg_col, slot_row, (q2, None), (pair, 0), (pair, 1), do2)
    p4 = dot_r(dq2, w_cross_q2).astype(BF16)
    pair_back = jnp.stack([dk2, dv2])
    cross = jnp.concatenate(
        [
            dot_t(n2, dq2).astype(BF16)[None],
            planes_grad(projected, pair_back),
            dot_t(e2, o2).astype(BF16)[None],
        ]
    )
    cross_part = lax.psum_scatter(cross, DP, scatter_dimension=1, tiled=True)
    dproj = planes_back(pair_back, w_kv2)
    (gain_one, shift_one, g1, e1), (dproj,) = run_flows(
        4,
        "query_sum",
        60,
        stream_flow(
            x1,
            norm_gains[1],
            terms=after(p4, cross),
            above=g2,
            rs=half,
            ag=half,
            clock=(5, 0, 6, 15),
            gather_clock=(37, 6),
        ),
        text_back_flow(dproj, half, n_tensor),
    )

    p6 = dot(after(act, e1), w_down).astype(BF16)
    down_sum = lax.psum_scatter(p6, TENSOR, scatter_dimension=0, tiled=True)
    image_out = (x2 + down_sum.astype(F32)).astype(BF16)

    do1 = dot_r(e1, w_self_out2).astype(BF16)
    dq1, dk1, dv1 = attend_back(seg_col, seg_row, (triple, 0), (triple, 1), (triple, 2), do1)
    triple_back = jnp.stack([dq1, dk1, dv1])
    own = planes_grad(n1, triple_back)
    own_out = dot_t(e1, o1).astype(BF16)[None]
    p5 = planes_back(triple_back, w_self2)
    text_w_part = dot_t(text, dproj).astype(BF16)
    p7 = dot_r(dproj, w_text).astype(BF16)
    everyone = [(TENSOR, bit) for bit in bits_of(n_tensor)] + [(DP, bit) for bit in bits_of(n_dp)]
    late = jnp.concatenate([gain_one, shift_one, gain_two, shift_two])
    (own, own_out), (unused, unused, image_grad, all_sums), (text_grad,), (cross,), (text_w,) = run_flows(
        5,
        "end",
        180,
        grads_flow((own, own_out), n_dp, half, clock=(20, 20)),
        stream_flow(
            image,
            norm_gains[0],
            terms=p5,
            above=g1,
            rs=half,
            keep=False,
            late=late,
            everyone=everyone,
            clock=(6, 0, 8, 50),
        ),
        stream_flow(terms=p7, rs=n_tensor, keep=False, clock=(7, 45, 11, 110)),
        grads_flow((cross_part,), n_dp, half, summing=False, clock=(15, 12)),
        grads_flow((text_w_part.reshape(4, -1, width),), n_dp, clock=(10, 16)),
    )
    self_grad = own.astype(F32)
    self_out_grad = own_out[0].astype(F32).T
    cross = cross.astype(F32)
    cross_q_grad = cross[0]
    cross_kv_grad = cross[1:3]
    cross_out_grad = cross[3].T
    text_w_grad = text_w.astype(F32).reshape(-1, width)
    down_grad, up_grad = [value.astype(F32) for value in sums]
    gain_grad = jnp.stack([all_sums[4], all_sums[0], all_sums[2]])
    shift_grad = jnp.stack([all_sums[5], all_sums[1], all_sums[3]])
    return (
        image_out,
        image_grad,
        text_grad,
        gain_grad,
        shift_grad,
        self_grad,
        self_out_grad,
        cross_q_grad,
        cross_kv_grad,
        cross_out_grad,
        text_w_grad,
        up_grad,
        down_grad,
    )


def solution(mesh):
    tokens = P((DP, TENSOR), None)
    columns = P(None, TENSOR)
    planes = P(None, None, TENSOR)
    rows = P(TENSOR, None)
    return jax.shard_map(
        local,
        mesh=mesh,
        in_specs=(
            tokens,
            P(DP, None),
            tokens,
            P(),
            P(),
            planes,
            rows,
            columns,
            planes,
            rows,
            columns,
            columns,
            rows,
            P(DP, None),
            P(DP),
        ),
        out_specs=(
            tokens,
            tokens,
            tokens,
            P(),
            P(),
            planes,
            rows,
            columns,
            planes,
            rows,
            columns,
            columns,
            rows,
        ),
        check_vma=False,
    )
```

```python
import functools

import jax
import jax.numpy as jnp
from jax import lax
from jax.experimental import pallas as pl
from jax.experimental.pallas import tpu as pltpu
from jax.sharding import PartitionSpec as P

HD = 128
IMGS = 4
CAP = 128
SCALE = HD ** (-0.5)
LOG2E = 1.4426950408889634
MIB = 1024 * 1024

epsilon = 1e-05
masked_value = -1e30

TENSOR = "tensor"
DP = "dp"

F32 = jnp.float32
BF16 = jnp.bfloat16


def raised_of(q, k, allowed):
    raw = lax.dot_general(q, k, (((1,), (1,)), ((), ())), preferred_element_type=F32)
    scores = jnp.where(allowed, raw * (SCALE * LOG2E), masked_value)
    raised = jnp.exp2(scores - jnp.max(scores, axis=-1, keepdims=True))
    return raised, 1.0 / jnp.sum(raised, axis=-1, keepdims=True)


def attend_kernel(step, qid_ref, kid_ref, q_ref, k_ref, v_ref, o_ref):
    k = k_ref[...]
    v = v_ref[...]
    kid = kid_ref[...]
    for start in range(0, q_ref.shape[0], step):
        rows = pl.ds(start, step)
        raised, rate = raised_of(q_ref[rows, :], k, qid_ref[rows, :] == kid)
        mixed = jnp.dot(raised.astype(BF16), v, preferred_element_type=F32)
        o_ref[rows, :] = (mixed * rate).astype(BF16)


def attend_back_kernel(step, qid_ref, kid_ref, q_ref, k_ref, v_ref, do_ref, dq_ref, dk_ref, dv_ref, dk_sum, dv_sum):
    k = k_ref[...]
    v = v_ref[...]
    kid = kid_ref[...]
    for start in range(0, q_ref.shape[0], step):
        rows = pl.ds(start, step)
        q = q_ref[rows, :]
        do = do_ref[rows, :]
        raised, rate = raised_of(q, k, qid_ref[rows, :] == kid)
        dp = lax.dot_general(do, v, (((1,), (1,)), ((), ())), preferred_element_type=F32)
        inner = jnp.sum(dp * raised, axis=-1, keepdims=True) * rate
        ds = (raised * ((dp - inner) * (rate * SCALE))).astype(BF16)
        dq_ref[rows, :] = jnp.dot(ds, k, preferred_element_type=F32).astype(BF16)
        dk = lax.dot_general(ds, q, (((0,), (0,)), ((), ())), preferred_element_type=F32)
        shared = (do.astype(F32) * rate).astype(BF16)
        dv = lax.dot_general(
            raised.astype(BF16), shared, (((0,), (0,)), ((), ())), preferred_element_type=F32
        )
        if start == 0:
            dk_sum[...] = dk
            dv_sum[...] = dv
        else:
            dk_sum[...] += dk
            dv_sum[...] += dv
    dk_ref[...] = dk_sum[...].astype(BF16)
    dv_ref[...] = dv_sum[...].astype(BF16)


def head_spec(rows, which):
    if which is None:
        return pl.BlockSpec((rows, HD), lambda h: (0, h))
    return pl.BlockSpec((None, rows, HD), lambda h: (which, 0, h))


def whole_spec(shape):
    return pl.BlockSpec(shape, lambda h: (0, 0))


def attend(qid, kid, query, keys, values):
    (qa, qp), (ka, kp), (va, vp) = query, keys, values
    tokens, width = qa.shape[-2:]
    slots = ka.shape[-2]
    heads = width // HD
    return pl.pallas_call(
        functools.partial(attend_kernel, 256),
        grid=(heads,),
        in_specs=[
            whole_spec(qid.shape),
            whole_spec(kid.shape),
            head_spec(tokens, qp),
            head_spec(slots, kp),
            head_spec(slots, vp),
        ],
        out_specs=head_spec(tokens, None),
        out_shape=jax.ShapeDtypeStruct((tokens, width), BF16),
        compiler_params=pltpu.CompilerParams(vmem_limit_bytes=48 * MIB),
        cost_estimate=pl.CostEstimate(
            flops=4 * tokens * slots * width,
            bytes_accessed=2 * width * (2 * tokens + 2 * slots),
            transcendentals=tokens * slots * heads,
        ),
        name="attend",
    )(qid, kid, qa, ka, va)


def attend_back(qid, kid, query, keys, values, do):
    (qa, qp), (ka, kp), (va, vp) = query, keys, values
    tokens, width = qa.shape[-2:]
    slots = ka.shape[-2]
    heads = width // HD
    return pl.pallas_call(
        functools.partial(attend_back_kernel, 256),
        grid=(heads,),
        in_specs=[
            whole_spec(qid.shape),
            whole_spec(kid.shape),
            head_spec(tokens, qp),
            head_spec(slots, kp),
            head_spec(slots, vp),
            head_spec(tokens, None),
        ],
        out_specs=[head_spec(tokens, None), head_spec(slots, None), head_spec(slots, None)],
        out_shape=[
            jax.ShapeDtypeStruct((tokens, width), BF16),
            jax.ShapeDtypeStruct((slots, width), BF16),
            jax.ShapeDtypeStruct((slots, width), BF16),
        ],
        scratch_shapes=[pltpu.VMEM((slots, HD), F32), pltpu.VMEM((slots, HD), F32)],
        compiler_params=pltpu.CompilerParams(vmem_limit_bytes=48 * MIB),
        cost_estimate=pl.CostEstimate(
            flops=10 * tokens * slots * width,
            bytes_accessed=2 * width * (3 * tokens + 4 * slots),
            transcendentals=tokens * slots * heads,
        ),
        name="attend_back",
    )(qid, kid, qa, ka, va, do)


def dot(left, right):
    return jnp.dot(left, right, preferred_element_type=F32)


def dot_t(left, right):
    return lax.dot_general(left, right, (((0,), (0,)), ((), ())), preferred_element_type=F32)


def dot_r(left, right):
    return lax.dot_general(left, right, (((1,), (1,)), ((), ())), preferred_element_type=F32)


def rows_dot_kernel(count, *refs):
    total = None
    for left_ref, right_ref in zip(refs[:count], refs[count : 2 * count]):
        term = lax.dot_general(
            left_ref[...], right_ref[...], (((1,), (1,)), ((), ())), preferred_element_type=F32
        )
        total = term if total is None else total + term
    refs[-1][...] = total.astype(BF16)


def rows_dot(lefts, right, tile=512):
    count = len(lefts)
    high, deep = lefts[0].shape
    wide = right.shape[1]
    return pl.pallas_call(
        functools.partial(rows_dot_kernel, count),
        grid=(wide // tile,),
        in_specs=[pl.BlockSpec((high, deep), lambda n: (0, 0))] * count
        + [pl.BlockSpec((None, tile, deep), lambda n, c=c: (c, n, 0)) for c in range(count)],
        out_specs=pl.BlockSpec((high, tile), lambda n: (0, n)),
        out_shape=jax.ShapeDtypeStruct((high, wide), BF16),
        compiler_params=pltpu.CompilerParams(vmem_limit_bytes=48 * MIB),
        cost_estimate=pl.CostEstimate(
            flops=2 * count * high * deep * wide,
            bytes_accessed=2 * (count * deep * (high + wide) + high * wide),
            transcendentals=0,
        ),
        name="rows_dot",
    )(*lefts, *[right] * count)


def columns_dot_kernel(left_ref, right_ref, out_ref):
    out_ref[...] = lax.dot_general(
        left_ref[...], right_ref[...], (((0,), (0,)), ((), ())), preferred_element_type=F32
    ).astype(BF16)


def columns_dot(left, right, tile=512):
    deep, high = left.shape
    wide = right.shape[1]
    return pl.pallas_call(
        columns_dot_kernel,
        grid=(high // tile,),
        in_specs=[
            pl.BlockSpec((deep, tile), lambda n: (0, n)),
            pl.BlockSpec((deep, wide), lambda n: (0, 0)),
        ],
        out_specs=pl.BlockSpec((tile, wide), lambda n: (n, 0)),
        out_shape=jax.ShapeDtypeStruct((high, wide), BF16),
        compiler_params=pltpu.CompilerParams(vmem_limit_bytes=48 * MIB),
        cost_estimate=pl.CostEstimate(
            flops=2 * deep * high * wide,
            bytes_accessed=2 * (deep * (high + wide) + high * wide),
            transcendentals=0,
        ),
        name="columns_dot",
    )(left, right)


def planes_of(left, right):
    return jnp.einsum("td,cde->cte", left, right, preferred_element_type=F32).astype(BF16)


def planes_grad(left, right):
    return jnp.einsum("td,cta->cda", left, right, preferred_element_type=F32).astype(BF16)


def planes_back(left, right):
    return jnp.einsum("cta,cda->td", left, right, preferred_element_type=F32).astype(BF16)


def norm_parts(value):
    mean = jnp.mean(value, axis=-1, keepdims=True)
    centered = value - mean
    spread = jnp.mean(centered * centered, axis=-1, keepdims=True)
    rate = lax.rsqrt(spread + epsilon)
    return centered * rate, rate


def gelu_parts(h):
    c = 0.7978845608028654
    inner = c * (h + 0.044715 * h * h * h)
    th = jnp.tanh(inner)
    half = 0.5 * (1.0 + th)
    slope = half + 0.5 * h * (1.0 - th * th) * (c * (1.0 + 3 * 0.044715 * h * h))
    return h * half, slope


def partner(index, bit):
    return index + bit - 2 * bit * ((index // bit) % 2)


def peer(index, mask):
    bit = 1
    while bit <= mask:
        if mask & bit:
            index = partner(index, bit)
        bit *= 2
    return index


def low_bit(value):
    return value & -value


def high_bit(value):
    return 1 << (value.bit_length() - 1)


def level_of(value):
    return sum((value >> i) & 1 for i in range(value.bit_length()))


def bits_of(size):
    return tuple(1 << i for i in range(size.bit_length() - 1))


def remote(src, dst, send_sem, recv_sem, axis, index):
    copy = pltpu.make_async_remote_copy(
        src_ref=src,
        dst_ref=dst,
        send_sem=send_sem,
        recv_sem=recv_sem,
        device_id={axis: index},
        device_id_type=pl.DeviceIdType.MESH,
    )
    copy.start()
    return copy


def local_copy(src, dst, sem):
    copy = pltpu.make_async_copy(src, dst, sem)
    copy.start()
    return copy


VMEM = pl.BlockSpec(memory_space=pltpu.VMEM)
HBM = pl.BlockSpec(memory_space=pl.ANY)
DMA = pltpu.SemaphoreType.DMA


class Flow:
    def __init__(self, partners):
        self.partners = partners
        self.ins, self.outs, self.scratch = [], [], []
        self.steps = None

    def take(self, array, spec=HBM):
        self.ins.append((array, spec))
        return (0, len(self.ins) - 1)

    def give(self, shape, dtype, spec=HBM):
        self.outs.append((jax.ShapeDtypeStruct(shape, dtype), spec))
        return (1, len(self.outs) - 1)

    def hold(self, kind):
        self.scratch.append((kind, None))
        return (2, len(self.scratch) - 1)

    def vmem(self, *shape, dtype=BF16):
        return self.hold(pltpu.VMEM(shape, dtype))

    def sems(self, *shape):
        return self.hold(DMA(shape))


def flows_kernel(flows, *refs):
    refs = list(refs)
    tables = [{} for unused in flows]
    for part in range(3):
        for flow, table in zip(flows, tables):
            for i in range(len((flow.ins, flow.outs, flow.scratch)[part])):
                table[part, i] = refs.pop(0)
    partners = []
    for flow in flows:
        partners += [entry for entry in flow.partners if entry not in partners]
    barrier = pltpu.get_barrier_semaphore()
    for axis, bit in partners:
        pl.semaphore_signal(
            barrier,
            inc=1,
            device_id={axis: partner(lax.axis_index(axis), bit)},
            device_id_type=pl.DeviceIdType.MESH,
        )
    pl.semaphore_wait(barrier, len(partners))
    running = [[0.0, flow.steps(table)] for flow, table in zip(flows, tables)]
    while running:
        entry = min(running, key=lambda e: e[0])
        moment = next(entry[1], None)
        if moment is None:
            running.remove(entry)
        else:
            entry[0] = moment


def run_flows(cid, name, micros, *flows):
    ins, outs, scratch = [
        [entry for flow in flows for entry in part(flow)]
        for part in (lambda f: f.ins, lambda f: f.outs, lambda f: f.scratch)
    ]
    results = pl.pallas_call(
        functools.partial(flows_kernel, flows),
        in_specs=[entry[1] for entry in ins],
        out_specs=[entry[1] for entry in outs],
        out_shape=[entry[0] for entry in outs],
        scratch_shapes=[entry[0] for entry in scratch],
        compiler_params=pltpu.CompilerParams(
            collective_id=cid, has_side_effects=True, vmem_limit_bytes=58 * MIB
        ),
        cost_estimate=pl.CostEstimate(
            flops=0, bytes_accessed=int(micros * 3.3e6), transcendentals=0
        ),
        name=name,
    )(*[entry[0] for entry in ins])
    results = list(results)
    return [tuple(results.pop(0) for unused in flow.outs) for flow in flows]


class Sum:
    def __init__(self, flow, size, chunks, high, wide):
        self.size, self.chunks = size, chunks
        self.held = flow.vmem(size // 2, high, wide)
        self.came = flow.vmem(size - 1, high, wide)
        self.load = flow.sems(size // 2, chunks)
        self.sent = flow.sems(size, chunks)
        self.got = flow.sems(size, chunks)

    def steps(self, r, view, rows, finish, clock):
        bits = bits_of(self.size)
        chunks = self.chunks
        index = lax.axis_index(TENSOR)
        held, came = r[self.held], r[self.came]
        firsts = sorted(range(0, self.size, 2), reverse=True)
        sent, loads = {}, {}

        def send(src, block, chunk, bit):
            sent[block, chunk] = remote(
                src,
                came.at[block - 1, rows(chunk)],
                r[self.sent].at[block, chunk],
                r[self.got].at[block, chunk],
                TENSOR,
                partner(index, bit),
            )

        def summed(block, chunk):
            loads[block, chunk].wait()
            total = held[block // 2, rows(chunk)].astype(F32)
            for bit in bits:
                if block == 0 or bit < low_bit(block):
                    sent[block + bit, chunk].wait_recv()
                    total = total + came[block + bit - 1, rows(chunk)].astype(F32)
            return total

        for block in firsts:
            for chunk in range(chunks):
                send(view(block + 1, chunk), block + 1, chunk, 1)
                loads[block, chunk] = local_copy(
                    view(block, chunk),
                    held.at[block // 2, rows(chunk)],
                    r[self.load].at[block // 2, chunk],
                )
        start, middle, pace, last = clock
        yield start
        for block in firsts:
            if block:
                for chunk in range(chunks):
                    if low_bit(block) > 2:
                        yield middle + chunk * pace
                    held[block // 2, rows(chunk)] = summed(block, chunk).astype(BF16)
                    send(held.at[block // 2, rows(chunk)], block, chunk, low_bit(block))
        for chunk in range(chunks):
            yield last + chunk * pace
            finish(chunk, summed(0, chunk))
        for copy in sent.values():
            copy.wait_send()


def norm_back_parts(value, gain, gradient):
    xh, rate = norm_parts(value)
    mg = gradient * gain
    back = rate * (
        mg - jnp.mean(mg, axis=-1, keepdims=True) - xh * jnp.mean(mg * xh, axis=-1, keepdims=True)
    )
    return back, jnp.sum(gradient * xh, axis=0, keepdims=True), jnp.sum(gradient, axis=0, keepdims=True)


def stream_flow(
    value=None,
    gain=None,
    shift=None,
    terms=None,
    above=None,
    rs=1,
    ag=1,
    keep=True,
    late=None,
    everyone=(),
    clock=(5, 30, 6, 60),
    gather_clock=(30, 6),
):
    if value is None:
        tokens, model = terms.shape[0] // rs, terms.shape[1]
    else:
        tokens, model = value.shape
    ag_bits = bits_of(ag)
    chunks = 4 if tokens % 64 == 0 else 1
    part = tokens // chunks
    flow = Flow([(TENSOR, bit) for bit in bits_of(max(rs, ag))] + list(everyone))
    if value is not None:
        value_key = flow.take(value, VMEM)
        gain_key = flow.take(gain[None], VMEM)
    if shift is not None:
        shift_key = flow.take(shift[None], VMEM)
    if above is not None:
        above_key = flow.take(above, VMEM)
        gain_sum = flow.give((1, model), F32, VMEM)
        shift_sum = flow.give((1, model), F32, VMEM)
    if rs > 1:
        terms_key = flow.take(terms)
        total_of = Sum(flow, rs, chunks, tokens, model)
    if keep:
        stream_key = flow.give((tokens, model), F32, VMEM)
    result_key = flow.give((ag * tokens, model), BF16, HBM if ag > 1 else VMEM)
    if ag > 1:
        own_key = flow.vmem(tokens, model)
        keep_sem = flow.sems(chunks)
        ag_send = flow.sems(ag, chunks)
        ag_recv = flow.sems(ag, chunks)
    if late is not None:
        late_key = flow.take(late, VMEM)
        all_key = flow.give((8, model), F32, VMEM)
        totals_key = flow.vmem(len(everyone) + 1, 8, model, dtype=F32)
        others_key = flow.vmem(len(everyone), 8, model, dtype=F32)
        totals_send = flow.sems(len(everyone))
        totals_recv = flow.sems(len(everyone))

    def rows(chunk):
        return pl.ds(chunk * part, part)

    def steps(r):
        t = lax.axis_index(TENSOR)

        def at(block, group, chunk):
            start = (peer(t, block) % group) * tokens + chunk * part
            return pl.ds(pl.multiple_of(start, 16), part)

        sent, keeps = {}, []

        def send(src, dst, block, chunk, bit):
            sent[block, chunk] = remote(
                src,
                dst,
                r[ag_send].at[block, chunk],
                r[ag_recv].at[block, chunk],
                TENSOR,
                partner(t, bit),
            )

        def finish(chunk, total):
            here = rows(chunk)
            if value is None:
                r[result_key][here, :] = total.astype(BF16)
                return
            stream = r[value_key][here, :].astype(F32)
            if above is None:
                if total is not None:
                    stream = stream + total
                    r[stream_key][here, :] = stream
                xh, unused = norm_parts(stream)
                result = (xh * r[gain_key][...] + r[shift_key][...]).astype(BF16)
            else:
                back, gains, shifts = norm_back_parts(stream, r[gain_key][...], total)
                if chunk == 0:
                    r[gain_sum][...] = gains
                    r[shift_sum][...] = shifts
                else:
                    r[gain_sum][...] += gains
                    r[shift_sum][...] += shifts
                gradient = r[above_key][here, :].astype(F32) + back
                if keep:
                    r[stream_key][here, :] = gradient
                result = gradient.astype(BF16)
            if ag == 1:
                r[result_key][here, :] = result
                return
            r[own_key][here, :] = result
            place = r[result_key].at[at(0, ag, chunk)]
            keeps.append(local_copy(r[own_key].at[here], place, r[keep_sem].at[chunk]))
            for bit in reversed(ag_bits):
                send(r[own_key].at[here], place, bit, chunk, bit)

        if rs > 1:
            yield from total_of.steps(
                r,
                lambda block, chunk: r[terms_key].at[at(block, rs, chunk)],
                rows,
                finish,
                clock,
            )
        else:
            for chunk in range(chunks):
                finish(chunk, None)
        if late is not None:
            count = late.shape[0]
            totals, others = r[totals_key], r[others_key]
            totals[0, :count] = r[late_key][...]
            totals[0, count : count + 1] = r[gain_sum][...]
            totals[0, count + 1 : count + 2] = r[shift_sum][...]
            totals[0, count + 2 :] = jnp.zeros_like(totals[0, count + 2 :])
            for i, (axis, bit) in enumerate(everyone):
                copy = remote(
                    totals.at[i],
                    others.at[i],
                    r[totals_send].at[i],
                    r[totals_recv].at[i],
                    axis,
                    partner(lax.axis_index(axis), bit),
                )
                yield clock[-1] + 40 + 15 * i
                copy.wait()
                totals[i + 1] = totals[i] + others[i]
            r[all_key][...] = totals[len(everyone)]
        first, pace = gather_clock
        for i, block in enumerate(sorted(range(2, ag, 2), key=lambda b: (level_of(b), low_bit(b)))):
            for chunk in range(chunks):
                yield first + (i * chunks + chunk) * pace
                sent[block, chunk].wait_recv()
                for bit in reversed(ag_bits):
                    if bit < low_bit(block):
                        place = r[result_key].at[at(block, ag, chunk)]
                        send(place, place, block + bit, chunk, bit)
        for (block, chunk), copy in sent.items():
            copy.wait_send()
            if block % 2:
                copy.wait_recv()
        for copy in keeps:
            copy.wait()

    flow.steps = steps
    return flow


def spread_on(side, block, bit):
    if block == 0:
        return True
    return bit < low_bit(block) if side == 0 else bit > high_bit(block)


def fetch_flow(weights, half, n_dp, window=3, clock=(8, 6.5)):
    dp_bits = bits_of(n_dp)
    units = [
        (which, plane, side)
        for which, (by_rows, weight) in enumerate(weights)
        for plane in range(weight.shape[0])
        for side in range(2)
    ]
    flow = Flow([(TENSOR, half)] + [(DP, bit) for bit in dp_bits])
    sources, targets, owns = [], [], []
    for by_rows, weight in weights:
        planes, high, wide = weight.shape
        sources.append(flow.take(weight))
        both = (planes, 2 * high, wide) if by_rows else (planes, high, 2 * wide)
        targets.append(flow.give(both, BF16))
        owns.append(flow.vmem(*weight.shape))
    sends = flow.sems(len(units), n_dp)
    recvs = flow.sems(len(units), n_dp)
    takes = flow.sems(len(weights))
    keep_sems = flow.sems(len(weights))

    def steps(r):
        t = lax.axis_index(TENSOR)
        d = lax.axis_index(DP)
        copies, keeps = {}, []

        def places(unit, block):
            which, plane, side = unit
            by_rows, weight = weights[which]
            source, target = r[sources[which]], r[targets[which]]
            high, wide = weight.shape[1:]
            size = (wide if by_rows else high) // n_dp // 2
            start = (peer(d, block) * 2 + side) * size
            if by_rows:
                columns = pl.ds(pl.multiple_of(start, 128), size)
                return source.at[plane, :, columns], target.at[plane, pl.ds(high, high), columns]
            rows = pl.ds(pl.multiple_of(start, 16), size)
            return source.at[plane, rows], target.at[plane, rows, pl.ds(wide, wide)]

        def send(src, dst, unit, block, axis, index):
            copies[unit, block] = remote(
                src, dst, r[sends].at[unit, block], r[recvs].at[unit, block], axis, index
            )

        def begin(unit):
            if unit < len(units):
                src, dst = places(units[unit], 0)
                send(src, dst, unit, 0, TENSOR, partner(t, half))

        def forward(unit, block):
            copies[unit, block].wait_recv()
            place = places(units[unit], block)[1]
            for bit in dp_bits:
                if spread_on(units[unit][2], block, bit):
                    send(place, place, unit, block + bit, DP, partner(d, bit))

        for unit in range(window):
            begin(unit)
        for which in range(len(weights)):
            keeps.append(local_copy(r[sources[which]], r[owns[which]], r[takes].at[which]))
        yield clock[0]
        for which, (by_rows, weight) in enumerate(weights):
            high, wide = weight.shape[1:]
            target = r[targets[which]]
            target = target.at[:, pl.ds(0, high)] if by_rows else target.at[:, :, pl.ds(0, wide)]
            keeps[which].wait()
            keeps[which] = local_copy(r[owns[which]], target, r[keep_sems].at[which])
        for step in range(len(units) + len(dp_bits) - 1):
            if step < len(units):
                forward(step, 0)
                begin(step + window)
            for level in range(1, len(dp_bits)):
                if 0 <= step - level < len(units):
                    for block in range(1, n_dp):
                        if level_of(block) == level:
                            forward(step - level, block)
            yield clock[0] + (step + 1) * clock[1]
        for unit in range(len(units)):
            copies[unit, n_dp - 1].wait_recv()
        for copy in copies.values():
            copy.wait_send()
        for copy in keeps:
            copy.wait()

    flow.steps = steps
    return flow


def text_flow(text, half, n, clock=(20, 12)):
    high, wide = text.shape[0] // (n // half), text.shape[1]
    flow = Flow([(TENSOR, bit) for bit in bits_of(n)])
    text_key = flow.take(text)
    result_key = flow.give((high, wide * n), BF16)
    own_key = flow.vmem(high, wide)
    sends, recvs, keeps = flow.sems(n), flow.sems(n), flow.sems(2)

    def steps(r):
        t = lax.axis_index(TENSOR)
        row = t // half
        copies = {}

        def rows(which):
            return r[text_key].at[pl.ds(pl.multiple_of(which * high, 16), high)]

        def columns(block):
            return r[result_key].at[:, pl.ds(pl.multiple_of(peer(t, block) * wide, 128), wide)]

        def send(src, dst, block, bit):
            copies[block] = remote(
                src, dst, r[sends].at[block], r[recvs].at[block], TENSOR, partner(t, bit)
            )

        for bit in reversed(bits_of(n)):
            send(rows(1 - row if bit == half else row), columns(0), bit, bit)
        keep = local_copy(rows(row), r[own_key], r[keeps].at[0])
        yield clock[0]
        keep.wait()
        keep = local_copy(r[own_key], columns(0), r[keeps].at[1])
        for i, block in enumerate(sorted(range(1, n), key=lambda b: (level_of(b), low_bit(b)))):
            copies[block].wait_recv()
            for bit in reversed(bits_of(n)):
                if bit < low_bit(block):
                    send(columns(block), columns(block), block + bit, bit)
            yield clock[0] + i * clock[1]
        for copy in copies.values():
            copy.wait_send()
        keep.wait()

    flow.steps = steps
    return flow


def text_back_flow(terms, half, n, clocks=((8, 30, 6, 30), (9, 30, 6, 35), 45)):
    high, wide = terms.shape[0], terms.shape[1] // n
    flow = Flow([(TENSOR, bit) for bit in bits_of(n)])
    terms_key = flow.take(terms)
    result_key = flow.give((high * (n // half), wide), BF16)
    sums = [Sum(flow, half, 1, high, wide) for unused in range(2)]
    owns = [flow.vmem(high, wide) for unused in range(2)]
    sems = flow.sems(3)

    def steps(r):
        t = lax.axis_index(TENSOR)
        row = t // half
        last = []

        def view(far):
            def place(block, chunk):
                column = peer(t, block + far) * wide
                return r[terms_key].at[:, pl.ds(pl.multiple_of(column, 128), wide)]

            return place

        def target():
            return r[result_key].at[pl.ds(pl.multiple_of(row * high, 16), high)]

        def finish_far(chunk, total):
            r[owns[0]][...] = total.astype(BF16)
            last.append(
                remote(
                    r[owns[0]],
                    target(),
                    r[sems].at[0],
                    r[sems].at[1],
                    TENSOR,
                    partner(t, half),
                )
            )

        def finish_near(chunk, total):
            r[owns[1]][...] = total.astype(BF16)
            last.append(local_copy(r[owns[1]], target(), r[sems].at[2]))

        def rows(chunk):
            return pl.ds(0, high)

        parts = [
            [0, sums[0].steps(r, view(half), rows, finish_far, clocks[0])],
            [0, sums[1].steps(r, view(0), rows, finish_near, clocks[1])],
        ]
        while parts:
            entry = min(parts, key=lambda e: e[0])
            if entry[0]:
                yield entry[0]
            moment = next(entry[1], None)
            if moment is None:
                parts.remove(entry)
            else:
                entry[0] = moment
        yield clocks[2]
        for copy in last:
            copy.wait()

    flow.steps = steps
    return flow


def grads_flow(grads, n_dp, outs, half=0, summing=True, window=4, clock=(10, 20), slack=1):
    high, whole = grads[0].shape[1:]
    high = high if summing else high * n_dp
    wide = whole // 2 if half else whole
    size = high // n_dp // 2
    dp_bits = bits_of(n_dp)
    units = [
        (which, plane, side)
        for which, grad in enumerate(grads)
        for plane in range(grad.shape[0])
        for side in range(2)
    ]
    count = len(units)
    depth = len(dp_bits)
    slots = n_dp // 2 if summing else 1
    flow = Flow([(DP, bit) for bit in dp_bits] + ([(TENSOR, half)] if half else []))
    sources = [flow.take(grad) for grad in grads]
    targets = [flow.give((n, high, wide) if n else (wide, high), BF16) for n in outs]
    target_of = [(i, plane) for i, n in enumerate(outs) for plane in range(max(n, 1))]
    flat = [(grad, plane) for grad in range(len(grads)) for plane in range(grads[grad].shape[0])]
    gathered = flow.vmem(len(flat), high, wide)
    turned = [unit for unit in range(count) if not outs[target_of[flat.index(units[unit][:2])][0]]]
    if turned:
        staged = flow.vmem(len(turned), n_dp, wide, size)
    if summing:
        held = flow.vmem(count, slots, size, whole)
    load_sems = flow.sems(count, slots)
    if summing:
        came = flow.vmem(count, n_dp - 1, size, whole)
        sum_send, sum_recv = flow.sems(count, n_dp), flow.sems(count, n_dp)
    if half:
        given = flow.vmem(count, size, wide)
        mid_send, mid_recv = flow.sems(count), flow.sems(count)
        if summing:
            mine = flow.vmem(count, size, wide, dtype=F32)
            theirs = flow.vmem(count, size, wide)
    ag_send, ag_recv = flow.sems(count, n_dp), flow.sems(count, n_dp)
    keep_sems = flow.sems(count, n_dp)

    def order(side):
        return dp_bits if side == 0 else tuple(reversed(dp_bits))

    def stage(side, block):
        return min(i for i, bit in enumerate(order(side)) if block & bit)

    def slot(side, block):
        return [b for b in range(n_dp) if b == 0 or stage(side, b) > 0].index(block)

    def steps(r):
        d = lax.axis_index(DP)
        sums, loads, mids, spreads, keeps = {}, {}, {}, {}, []

        def rows_of(unit, block):
            return pl.ds(pl.multiple_of((peer(d, block) * 2 + units[unit][2]) * size, 16), size)

        def source_of(unit, block):
            which, plane, side = units[unit]
            rows = rows_of(unit, block) if summing else pl.ds(side * size, size)
            return r[sources[which]].at[plane, rows]

        def region(unit, block):
            return r[gathered].at[flat.index(units[unit][:2]), rows_of(unit, block)]

        def swap(src, unit):
            mids[unit] = remote(
                src,
                r[given].at[unit],
                r[mid_send].at[unit],
                r[mid_recv].at[unit],
                TENSOR,
                partner(lax.axis_index(TENSOR), half),
            )

        def send(src, unit, block):
            side = units[unit][2]
            sums[unit, block] = remote(
                src,
                r[came].at[unit, block - 1],
                r[sum_send].at[unit, block],
                r[sum_recv].at[unit, block],
                DP,
                partner(d, order(side)[stage(side, block)]),
            )

        def summed(unit, block):
            side = units[unit][2]
            loads[unit, block].wait()
            total = r[held][unit, slot(side, block)].astype(F32)
            for i, bit in enumerate(order(side)):
                if summing and (block == 0 or i < stage(side, block)):
                    sums[unit, block + bit].wait_recv()
                    total = total + r[came][unit, block + bit - 1].astype(F32)
            return total

        def begin(unit):
            if unit >= count:
                return
            side = units[unit][2]
            if not summing:
                source = source_of(unit, 0)
                swap(source.at[:, pl.ds(wide, wide)], unit)
                loads[unit, 0] = local_copy(
                    source.at[:, pl.ds(0, wide)], region(unit, 0), r[load_sems].at[unit, 0]
                )
                return
            for block in range(n_dp):
                source = source_of(unit, block)
                if block and stage(side, block) == 0:
                    send(source, unit, block)
                else:
                    place = slot(side, block)
                    loads[unit, block] = local_copy(
                        source, r[held].at[unit, place], r[load_sems].at[unit, place]
                    )

        def middle(unit, level):
            side = units[unit][2]
            for block in range(1, n_dp):
                if stage(side, block) == level:
                    r[held][unit, slot(side, block)] = summed(unit, block).astype(BF16)
                    send(r[held].at[unit, slot(side, block)], unit, block)

        def cross(unit):
            if half and summing:
                total = summed(unit, 0)
                r[mine][unit] = total[:, :wide]
                r[theirs][unit] = total[:, wide:].astype(BF16)
                swap(r[theirs].at[unit], unit)

        def spread(unit, block, src, dst):
            for bit in dp_bits:
                if spread_on(units[unit][2], block, bit):
                    spreads[unit, block + bit] = remote(
                        src,
                        dst,
                        r[ag_send].at[unit, block + bit],
                        r[ag_recv].at[unit, block + bit],
                        DP,
                        partner(d, bit),
                    )

        def settle(unit):
            place = region(unit, 0)
            if half and summing:
                total = r[mine][unit]
            elif summing:
                total = summed(unit, 0)
            else:
                loads[unit, 0].wait()
                total = place[...].astype(F32)
            if half:
                mids[unit].wait_recv()
                total = total + r[given][unit].astype(F32)
            place[...] = total.astype(BF16)
            spread(unit, 0, place, place)

        def onward(unit, level):
            for block in range(1, n_dp):
                if level_of(block) == level:
                    spreads[unit, block].wait_recv()
                    place = region(unit, block)
                    spread(unit, block, place, place)

        def write(unit):
            spreads[unit, n_dp - 1].wait_recv()
            which, plane = target_of[flat.index(units[unit][:2])]
            target = r[targets[which]]
            for block in range(n_dp):
                src = region(unit, block)
                if outs[which]:
                    to = target.at[plane, rows_of(unit, block)]
                else:
                    place = turned.index(unit)
                    r[staged][place, block] = src[...].astype(F32).T.astype(BF16)
                    src = r[staged].at[place, block]
                    start = (peer(d, block) * 2 + units[unit][2]) * size
                    to = target.at[:, pl.ds(pl.multiple_of(start, 128), size)]
                keeps.append(local_copy(src, to, r[keep_sems].at[unit, block]))

        for unit in range(window):
            begin(unit)
        start = max(depth - 1, 0) if summing else 0
        first = start + (1 if summing else 0) + (slack if half else 0)
        for step in range(count + first + depth):
            yield clock[0] + step * clock[1]

            def turn(lag, action, *more):
                if 0 <= step - lag < count:
                    action(step - lag, *more)

            turn(first + depth, write)

            for level in range(depth - 1, 0, -1):
                turn(first + level, onward, level)
            turn(first, settle)
            turn(start, cross)
            if summing:
                for level in range(depth - 1, 0, -1):
                    turn(level - 1, middle, level)
            begin(step + window)
        for copy in [*sums.values(), *mids.values(), *spreads.values()]:
            copy.wait_send()
        for copy in keeps:
            copy.wait()

    flow.steps = steps
    return flow


def dot_flow(left, right, turned=False, parts=8, clock=(4, 8)):
    flow = Flow([])
    high, deep = left.shape
    wide = right.shape[0] if turned else right.shape[1]
    part = high // parts
    left_key, right_key = flow.take(left), flow.take(right)
    result_key = flow.give((high, wide), BF16)
    lefts, rights = flow.vmem(2, part, deep), flow.vmem(*right.shape)
    results = flow.vmem(2, part, wide)
    sems, right_sem = flow.sems(2, 2), flow.sems(1)

    def steps(r):
        loads, stores = {}, {}

        def load(i):
            if i < parts:
                loads[i] = local_copy(
                    r[left_key].at[pl.ds(i * part, part)], r[lefts].at[i % 2], r[sems].at[0, i % 2]
                )

        whole = local_copy(r[right_key], r[rights], r[right_sem].at[0])
        load(0)
        load(1)
        for i in range(parts):
            yield clock[0] + i * clock[1]
            if i == 0:
                whole.wait()
            loads[i].wait()
            if i > 1:
                stores[i - 2].wait()
            dims = (((1,), (1 if turned else 0,)), ((), ()))
            value = lax.dot_general(
                r[lefts][i % 2], r[rights][...], dims, preferred_element_type=F32
            )
            r[results][i % 2] = value.astype(BF16)
            stores[i] = local_copy(
                r[results].at[i % 2], r[result_key].at[pl.ds(i * part, part)], r[sems].at[1, i % 2]
            )
            load(i + 2)
        for i in range(max(parts - 2, 0), parts):
            stores[i].wait()

    flow.steps = steps
    return flow


def pass_flow(value):
    flow = Flow([])
    value_key = flow.take(value)
    result_key = flow.give(value.shape, value.dtype)
    held = flow.vmem(*value.shape)
    sems = flow.sems(2)

    def steps(r):
        copy = local_copy(r[value_key], r[held], r[sems].at[0])
        yield 8
        copy.wait()
        copy = local_copy(r[held], r[result_key], r[sems].at[1])
        yield 30
        copy.wait()

    flow.steps = steps
    return flow


def nothing(*refs):
    pass


def after(value, *before):
    return pl.pallas_call(
        nothing,
        in_specs=[HBM] * (1 + len(before)),
        out_specs=HBM,
        out_shape=jax.ShapeDtypeStruct(value.shape, value.dtype),
        input_output_aliases={0: 0},
    )(value, *before)


def local(
    image,
    text,
    cotangent,
    norm_gains,
    norm_shifts,
    w_self,
    w_self_out,
    w_cross_q,
    w_cross_kv,
    w_cross_out,
    w_text,
    w_up,
    w_down,
    segment_ids,
    caption_lengths,
):
    rows_here = segment_ids.shape[0]
    n_tensor = lax.axis_size(TENSOR)
    n_dp = lax.axis_size(DP)
    half = n_tensor // rows_here
    row = lax.axis_index(TENSOR) // half
    width = w_self.shape[2]
    slots = IMGS * CAP

    seg = lax.dynamic_index_in_dim(segment_ids, row, 0, keepdims=False)
    seg_col = seg[:, None]
    seg_row = seg[None, :]
    lengths = lax.dynamic_index_in_dim(caption_lengths.reshape(rows_here, IMGS), row, 0, keepdims=False)
    slot = jnp.arange(slots, dtype=jnp.int32)
    live = (slot % CAP) < jnp.repeat(lengths, CAP)
    slot_row = jnp.where(live, slot // CAP, -1)[None, :]

    (w_self2, w_self_out2), (n1,), (later,), (text_columns,) = run_flows(
        0,
        "start",
        60,
        fetch_flow(((False, w_self), (True, w_self_out[None])), half, n_dp),
        stream_flow(
            image, norm_gains[0], norm_shifts[0], ag=half, keep=False, gather_clock=(12, 11)
        ),
        pass_flow(cotangent),
        dot_flow(text, w_text),
    )
    w_self_out2 = w_self_out2[0]
    triple = planes_of(n1, w_self2)
    o1 = attend(seg_col, seg_row, (triple, 0), (triple, 1), (triple, 2))
    p1 = dot(o1, w_self_out2).astype(BF16)
    e3 = lax.all_gather(later, TENSOR, axis=0, tiled=True)
    (x1, n2), (w_kv2, w_cross_q2, w_cross_out2), (projected,) = run_flows(
        1,
        "self_sum",
        100,
        stream_flow(
            image,
            norm_gains[1],
            norm_shifts[1],
            terms=p1,
            rs=half,
            ag=half,
            clock=(5, 0, 10, 18),
            gather_clock=(60, 10),
        ),
        fetch_flow(
            ((False, w_cross_kv), (False, w_cross_q[None]), (True, w_cross_out[None])),
            half,
            n_dp,
            clock=(20, 8),
        ),
        text_flow(text_columns, half, n_tensor),
    )
    w_cross_q2, w_cross_out2 = w_cross_q2[0], w_cross_out2[0]

    pair = planes_of(projected, w_kv2)
    q2 = dot(n2, w_cross_q2).astype(BF16)
    o2 = attend(seg_col, slot_row, (q2, None), (pair, 0), (pair, 1))
    p2 = dot(o2, w_cross_out2).astype(BF16)
    (x2, n3), (active_back,) = run_flows(
        2,
        "cross_sum",
        100,
        stream_flow(
            x1,
            norm_gains[2],
            norm_shifts[2],
            terms=p2,
            rs=half,
            ag=n_tensor,
            clock=(5, 0, 6, 15),
            gather_clock=(40, 6),
        ),
        dot_flow(e3, w_down, True, clock=(4, 11)),
    )

    act, slope = gelu_parts(dot(n3, w_up))
    act = act.astype(BF16)
    dh = (active_back.astype(F32) * slope).astype(BF16)
    down_grad = dot_t(act, e3).astype(BF16)
    up_grad = dot_t(n3, dh).astype(BF16)
    sums = lax.psum((down_grad, up_grad), DP)
    p3 = after(rows_dot([dh], w_up[None]), down_grad, up_grad)
    (gain_two, shift_two, g2, e2), (p6,) = run_flows(
        3,
        "up_sum",
        100,
        stream_flow(
            x2, norm_gains[2], terms=p3, above=cotangent, rs=n_tensor, ag=half, clock=(8, 30, 6, 60)
        ),
        dot_flow(act, w_down, clock=(12, 10)),
    )

    do2 = dot_r(e2, w_cross_out2).astype(BF16)
    dq2, dk2, dv2 = attend_back(seg_col, slot_row, (q2, None), (pair, 0), (pair, 1), do2)
    p4 = rows_dot([dq2], w_cross_q2[None])
    pair_back = jnp.stack([dk2, dv2])
    cross = jnp.concatenate(
        [
            dot_t(n2, dq2).astype(BF16)[None],
            planes_grad(projected, pair_back),
            dot_t(e2, o2).astype(BF16)[None],
        ]
    )
    cross_part = lax.psum_scatter(cross, DP, scatter_dimension=1, tiled=True)
    dproj = rows_dot([dk2, dv2], w_kv2)
    (gain_one, shift_one, g1, e1), (dproj,) = run_flows(
        4,
        "query_sum",
        60,
        stream_flow(
            x1,
            norm_gains[1],
            terms=after(p4, cross),
            above=g2,
            rs=half,
            ag=half,
            clock=(5, 0, 6, 15),
            gather_clock=(37, 6),
        ),
        text_back_flow(dproj, half, n_tensor),
    )

    down_sum = lax.psum_scatter(after(p6, e1), TENSOR, scatter_dimension=0, tiled=True)
    image_out = (x2 + down_sum.astype(F32)).astype(BF16)

    do1 = dot_r(e1, w_self_out2).astype(BF16)
    dq1, dk1, dv1 = attend_back(seg_col, seg_row, (triple, 0), (triple, 1), (triple, 2), do1)
    triple_back = jnp.stack([dq1, dk1, dv1])
    own = planes_grad(n1, triple_back)
    own_out = dot_t(e1, o1).astype(BF16)[None]
    p5 = planes_back(triple_back, w_self2)
    text_w_part = columns_dot(text, dproj)
    p7 = rows_dot([dproj], w_text[None], 1024)
    everyone = [(TENSOR, bit) for bit in bits_of(n_tensor)] + [(DP, bit) for bit in bits_of(n_dp)]
    late = jnp.concatenate([gain_one, shift_one, gain_two, shift_two])
    (
        (self_grad, self_out_grad),
        (unused, unused, image_grad, all_sums),
        (text_grad,),
        (cross_q_grad, cross_kv_grad, cross_out_grad),
        (text_w_grad,),
    ) = run_flows(
        5,
        "end",
        200,
        grads_flow((own, own_out), n_dp, (3, 0), half, clock=(14, 14)),
        stream_flow(
            image,
            norm_gains[0],
            terms=p5,
            above=g1,
            rs=half,
            keep=False,
            late=late,
            everyone=everyone,
            clock=(6, 0, 8, 50),
        ),
        stream_flow(terms=p7, rs=n_tensor, keep=False, clock=(7, 45, 11, 110)),
        grads_flow((cross_part,), n_dp, (1, 2, 0), half, summing=False, clock=(15, 12)),
        grads_flow((text_w_part.reshape(4, -1, width),), n_dp, (4,), clock=(10, 16)),
    )
    down_grad, up_grad = [value.astype(F32) for value in sums]
    self_grad, self_out_grad = self_grad.astype(F32), self_out_grad.astype(F32)
    cross_q_grad, cross_kv_grad = cross_q_grad[0].astype(F32), cross_kv_grad.astype(F32)
    cross_out_grad = cross_out_grad.astype(F32)
    text_w_grad = text_w_grad.reshape(-1, width).astype(F32)
    gain_grad = jnp.stack([all_sums[4], all_sums[0], all_sums[2]])
    shift_grad = jnp.stack([all_sums[5], all_sums[1], all_sums[3]])
    return (
        image_out,
        image_grad,
        text_grad,
        gain_grad,
        shift_grad,
        self_grad,
        self_out_grad,
        cross_q_grad,
        cross_kv_grad,
        cross_out_grad,
        text_w_grad,
        up_grad,
        down_grad,
    )


def solution(mesh):
    tokens = P((DP, TENSOR), None)
    columns = P(None, TENSOR)
    planes = P(None, None, TENSOR)
    rows = P(TENSOR, None)
    return jax.shard_map(
        local,
        mesh=mesh,
        in_specs=(
            tokens,
            P(DP, None),
            tokens,
            P(),
            P(),
            planes,
            rows,
            columns,
            planes,
            rows,
            columns,
            columns,
            rows,
            P(DP, None),
            P(DP),
        ),
        out_specs=(
            tokens,
            tokens,
            tokens,
            P(),
            P(),
            planes,
            rows,
            columns,
            planes,
            rows,
            columns,
            columns,
            rows,
        ),
        check_vma=False,
    )
```

```python
import functools

import jax
import jax.numpy as jnp
from jax import lax
from jax.experimental import pallas as pl
from jax.experimental.pallas import tpu as pltpu
from jax.sharding import PartitionSpec as P

HD = 128
IMGS = 4
CAP = 128
SCALE = HD ** (-0.5)
LOG2E = 1.4426950408889634
MIB = 1024 * 1024

epsilon = 1e-05
masked_value = -1e30

TENSOR = "tensor"
DP = "dp"

F32 = jnp.float32
BF16 = jnp.bfloat16


def raised_of(q, k, allowed):
    raw = lax.dot_general(q, k, (((1,), (1,)), ((), ())), preferred_element_type=F32)
    scores = jnp.where(allowed, raw * (SCALE * LOG2E), masked_value)
    raised = jnp.exp2(scores - jnp.max(scores, axis=-1, keepdims=True))
    return raised, 1.0 / jnp.sum(raised, axis=-1, keepdims=True)


def attend_kernel(step, qid_ref, kid_ref, q_ref, k_ref, v_ref, o_ref):
    k = k_ref[...]
    v = v_ref[...]
    kid = kid_ref[...]
    for start in range(0, q_ref.shape[0], step):
        rows = pl.ds(start, step)
        raised, rate = raised_of(q_ref[rows, :], k, qid_ref[rows, :] == kid)
        mixed = jnp.dot(raised.astype(BF16), v, preferred_element_type=F32)
        o_ref[rows, :] = (mixed * rate).astype(BF16)


def attend_back_kernel(step, qid_ref, kid_ref, q_ref, k_ref, v_ref, do_ref, dq_ref, dk_ref, dv_ref, dk_sum, dv_sum):
    k = k_ref[...]
    v = v_ref[...]
    kid = kid_ref[...]
    for start in range(0, q_ref.shape[0], step):
        rows = pl.ds(start, step)
        q = q_ref[rows, :]
        do = do_ref[rows, :]
        raised, rate = raised_of(q, k, qid_ref[rows, :] == kid)
        dp = lax.dot_general(do, v, (((1,), (1,)), ((), ())), preferred_element_type=F32)
        inner = jnp.sum(dp * raised, axis=-1, keepdims=True) * rate
        ds = (raised * ((dp - inner) * (rate * SCALE))).astype(BF16)
        dq_ref[rows, :] = jnp.dot(ds, k, preferred_element_type=F32).astype(BF16)
        dk = lax.dot_general(ds, q, (((0,), (0,)), ((), ())), preferred_element_type=F32)
        shared = (do.astype(F32) * rate).astype(BF16)
        dv = lax.dot_general(
            raised.astype(BF16), shared, (((0,), (0,)), ((), ())), preferred_element_type=F32
        )
        if start == 0:
            dk_sum[...] = dk
            dv_sum[...] = dv
        else:
            dk_sum[...] += dk
            dv_sum[...] += dv
    dk_ref[...] = dk_sum[...].astype(BF16)
    dv_ref[...] = dv_sum[...].astype(BF16)


def head_spec(rows, which):
    if which is None:
        return pl.BlockSpec((rows, HD), lambda h: (0, h))
    return pl.BlockSpec((None, rows, HD), lambda h: (which, 0, h))


def whole_spec(shape):
    return pl.BlockSpec(shape, lambda h: (0, 0))


def attend(qid, kid, query, keys, values):
    (qa, qp), (ka, kp), (va, vp) = query, keys, values
    tokens, width = qa.shape[-2:]
    slots = ka.shape[-2]
    heads = width // HD
    return pl.pallas_call(
        functools.partial(attend_kernel, 256),
        grid=(heads,),
        in_specs=[
            whole_spec(qid.shape),
            whole_spec(kid.shape),
            head_spec(tokens, qp),
            head_spec(slots, kp),
            head_spec(slots, vp),
        ],
        out_specs=head_spec(tokens, None),
        out_shape=jax.ShapeDtypeStruct((tokens, width), BF16),
        compiler_params=pltpu.CompilerParams(vmem_limit_bytes=48 * MIB),
        cost_estimate=pl.CostEstimate(
            flops=4 * tokens * slots * width,
            bytes_accessed=2 * width * (2 * tokens + 2 * slots),
            transcendentals=tokens * slots * heads,
        ),
        name="attend",
    )(qid, kid, qa, ka, va)


def attend_back(qid, kid, query, keys, values, do):
    (qa, qp), (ka, kp), (va, vp) = query, keys, values
    tokens, width = qa.shape[-2:]
    slots = ka.shape[-2]
    heads = width // HD
    return pl.pallas_call(
        functools.partial(attend_back_kernel, 256),
        grid=(heads,),
        in_specs=[
            whole_spec(qid.shape),
            whole_spec(kid.shape),
            head_spec(tokens, qp),
            head_spec(slots, kp),
            head_spec(slots, vp),
            head_spec(tokens, None),
        ],
        out_specs=[head_spec(tokens, None), head_spec(slots, None), head_spec(slots, None)],
        out_shape=[
            jax.ShapeDtypeStruct((tokens, width), BF16),
            jax.ShapeDtypeStruct((slots, width), BF16),
            jax.ShapeDtypeStruct((slots, width), BF16),
        ],
        scratch_shapes=[pltpu.VMEM((slots, HD), F32), pltpu.VMEM((slots, HD), F32)],
        compiler_params=pltpu.CompilerParams(vmem_limit_bytes=48 * MIB),
        cost_estimate=pl.CostEstimate(
            flops=10 * tokens * slots * width,
            bytes_accessed=2 * width * (3 * tokens + 4 * slots),
            transcendentals=tokens * slots * heads,
        ),
        name="attend_back",
    )(qid, kid, qa, ka, va, do)


def dot(left, right):
    return jnp.dot(left, right, preferred_element_type=F32)


def dot_t(left, right):
    return lax.dot_general(left, right, (((0,), (0,)), ((), ())), preferred_element_type=F32)


def dot_r(left, right):
    return lax.dot_general(left, right, (((1,), (1,)), ((), ())), preferred_element_type=F32)


def rows_dot_kernel(count, *refs):
    total = None
    for left_ref, right_ref in zip(refs[:count], refs[count : 2 * count]):
        term = lax.dot_general(
            left_ref[...], right_ref[...], (((1,), (1,)), ((), ())), preferred_element_type=F32
        )
        total = term if total is None else total + term
    refs[-1][...] = total.astype(BF16)


def rows_dot(lefts, right, tile=512):
    count = len(lefts)
    high, deep = lefts[0].shape
    wide = right.shape[1]
    return pl.pallas_call(
        functools.partial(rows_dot_kernel, count),
        grid=(wide // tile,),
        in_specs=[pl.BlockSpec((high, deep), lambda n: (0, 0))] * count
        + [pl.BlockSpec((None, tile, deep), lambda n, c=c: (c, n, 0)) for c in range(count)],
        out_specs=pl.BlockSpec((high, tile), lambda n: (0, n)),
        out_shape=jax.ShapeDtypeStruct((high, wide), BF16),
        compiler_params=pltpu.CompilerParams(vmem_limit_bytes=48 * MIB),
        cost_estimate=pl.CostEstimate(
            flops=2 * count * high * deep * wide,
            bytes_accessed=2 * (count * deep * (high + wide) + high * wide),
            transcendentals=0,
        ),
        name="rows_dot",
    )(*lefts, *[right] * count)


def columns_dot_kernel(left_ref, right_ref, out_ref):
    out_ref[...] = lax.dot_general(
        left_ref[...], right_ref[...], (((0,), (0,)), ((), ())), preferred_element_type=F32
    ).astype(BF16)


def columns_dot(left, right, tile=512):
    deep, high = left.shape
    wide = right.shape[1]
    return pl.pallas_call(
        columns_dot_kernel,
        grid=(high // tile,),
        in_specs=[
            pl.BlockSpec((deep, tile), lambda n: (0, n)),
            pl.BlockSpec((deep, wide), lambda n: (0, 0)),
        ],
        out_specs=pl.BlockSpec((tile, wide), lambda n: (n, 0)),
        out_shape=jax.ShapeDtypeStruct((high, wide), BF16),
        compiler_params=pltpu.CompilerParams(vmem_limit_bytes=48 * MIB),
        cost_estimate=pl.CostEstimate(
            flops=2 * deep * high * wide,
            bytes_accessed=2 * (deep * (high + wide) + high * wide),
            transcendentals=0,
        ),
        name="columns_dot",
    )(left, right)


def planes_of(left, right):
    return jnp.einsum("td,cde->cte", left, right, preferred_element_type=F32).astype(BF16)


def planes_grad(left, right):
    return jnp.einsum("td,cta->cda", left, right, preferred_element_type=F32).astype(BF16)


def planes_back(left, right):
    return jnp.einsum("cta,cda->td", left, right, preferred_element_type=F32).astype(BF16)


def norm_parts(value):
    mean = jnp.mean(value, axis=-1, keepdims=True)
    centered = value - mean
    spread = jnp.mean(centered * centered, axis=-1, keepdims=True)
    rate = lax.rsqrt(spread + epsilon)
    return centered * rate, rate


def gelu_parts(h):
    c = 0.7978845608028654
    inner = c * (h + 0.044715 * h * h * h)
    th = jnp.tanh(inner)
    half = 0.5 * (1.0 + th)
    slope = half + 0.5 * h * (1.0 - th * th) * (c * (1.0 + 3 * 0.044715 * h * h))
    return h * half, slope


def hidden_kernel(tokens_ref, weight_ref, back_ref, act_ref, out_ref):
    h = jnp.dot(tokens_ref[...], weight_ref[...], preferred_element_type=F32)
    act, slope = gelu_parts(h)
    act_ref[...] = act.astype(BF16)
    out_ref[...] = (back_ref[...].astype(F32) * slope).astype(BF16)


def hidden_step(tokens, weight, back, tile=256):
    high, deep = tokens.shape
    wide = weight.shape[1]
    part = pl.BlockSpec((tile, wide), lambda m: (m, 0))
    return pl.pallas_call(
        hidden_kernel,
        grid=(high // tile,),
        in_specs=[
            pl.BlockSpec((tile, deep), lambda m: (m, 0)),
            pl.BlockSpec((deep, wide), lambda m: (0, 0)),
            part,
        ],
        out_specs=[part, part],
        out_shape=[jax.ShapeDtypeStruct((high, wide), BF16)] * 2,
        compiler_params=pltpu.CompilerParams(vmem_limit_bytes=48 * MIB),
        cost_estimate=pl.CostEstimate(
            flops=2 * high * deep * wide,
            bytes_accessed=2 * (high * deep + deep * wide + 3 * high * wide),
            transcendentals=high * wide,
        ),
        name="hidden_step",
    )(tokens, weight, back)


def partner(index, bit):
    return index + bit - 2 * bit * ((index // bit) % 2)


def peer(index, mask):
    bit = 1
    while bit <= mask:
        if mask & bit:
            index = partner(index, bit)
        bit *= 2
    return index


def low_bit(value):
    return value & -value


def high_bit(value):
    return 1 << (value.bit_length() - 1)


def level_of(value):
    return sum((value >> i) & 1 for i in range(value.bit_length()))


def bits_of(size):
    return tuple(1 << i for i in range(size.bit_length() - 1))


def remote(src, dst, send_sem, recv_sem, axis, index):
    copy = pltpu.make_async_remote_copy(
        src_ref=src,
        dst_ref=dst,
        send_sem=send_sem,
        recv_sem=recv_sem,
        device_id={axis: index},
        device_id_type=pl.DeviceIdType.MESH,
    )
    copy.start()
    return copy


def local_copy(src, dst, sem):
    copy = pltpu.make_async_copy(src, dst, sem)
    copy.start()
    return copy


VMEM = pl.BlockSpec(memory_space=pltpu.VMEM)
HBM = pl.BlockSpec(memory_space=pl.ANY)
DMA = pltpu.SemaphoreType.DMA


class Flow:
    def __init__(self, partners):
        self.partners = partners
        self.ins, self.outs, self.scratch = [], [], []
        self.steps = None

    def take(self, array, spec=HBM):
        self.ins.append((array, spec))
        return (0, len(self.ins) - 1)

    def give(self, shape, dtype, spec=HBM):
        self.outs.append((jax.ShapeDtypeStruct(shape, dtype), spec))
        return (1, len(self.outs) - 1)

    def hold(self, kind):
        self.scratch.append((kind, None))
        return (2, len(self.scratch) - 1)

    def vmem(self, *shape, dtype=BF16):
        return self.hold(pltpu.VMEM(shape, dtype))

    def sems(self, *shape):
        return self.hold(DMA(shape))


def flows_kernel(flows, *refs):
    refs = list(refs)
    tables = [{} for unused in flows]
    for part in range(3):
        for flow, table in zip(flows, tables):
            for i in range(len((flow.ins, flow.outs, flow.scratch)[part])):
                table[part, i] = refs.pop(0)
    partners = []
    for flow in flows:
        partners += [entry for entry in flow.partners if entry not in partners]
    barrier = pltpu.get_barrier_semaphore()
    for axis, bit in partners:
        pl.semaphore_signal(
            barrier,
            inc=1,
            device_id={axis: partner(lax.axis_index(axis), bit)},
            device_id_type=pl.DeviceIdType.MESH,
        )
    pl.semaphore_wait(barrier, len(partners))
    running = [[0.0, flow.steps(table)] for flow, table in zip(flows, tables)]
    while running:
        entry = min(running, key=lambda e: e[0])
        moment = next(entry[1], None)
        if moment is None:
            running.remove(entry)
        else:
            entry[0] = moment


def run_flows(cid, name, micros, *flows):
    ins, outs, scratch = [
        [entry for flow in flows for entry in part(flow)]
        for part in (lambda f: f.ins, lambda f: f.outs, lambda f: f.scratch)
    ]
    results = pl.pallas_call(
        functools.partial(flows_kernel, flows),
        in_specs=[entry[1] for entry in ins],
        out_specs=[entry[1] for entry in outs],
        out_shape=[entry[0] for entry in outs],
        scratch_shapes=[entry[0] for entry in scratch],
        compiler_params=pltpu.CompilerParams(
            collective_id=cid, has_side_effects=True, vmem_limit_bytes=58 * MIB
        ),
        cost_estimate=pl.CostEstimate(
            flops=0, bytes_accessed=int(micros * 3.3e6), transcendentals=0
        ),
        name=name,
    )(*[entry[0] for entry in ins])
    results = list(results)
    return [tuple(results.pop(0) for unused in flow.outs) for flow in flows]


class Sum:
    def __init__(self, flow, size, chunks, high, wide):
        self.size, self.chunks = size, chunks
        self.held = flow.vmem(size // 2, high, wide)
        self.came = flow.vmem(size - 1, high, wide)
        self.load = flow.sems(size // 2, chunks)
        self.sent = flow.sems(size, chunks)
        self.got = flow.sems(size, chunks)

    def steps(self, r, view, rows, finish, clock):
        bits = bits_of(self.size)
        chunks = self.chunks
        index = lax.axis_index(TENSOR)
        held, came = r[self.held], r[self.came]
        firsts = sorted(range(0, self.size, 2), reverse=True)
        sent, loads = {}, {}

        def send(src, block, chunk, bit):
            sent[block, chunk] = remote(
                src,
                came.at[block - 1, rows(chunk)],
                r[self.sent].at[block, chunk],
                r[self.got].at[block, chunk],
                TENSOR,
                partner(index, bit),
            )

        def summed(block, chunk):
            loads[block, chunk].wait()
            total = held[block // 2, rows(chunk)].astype(F32)
            for bit in bits:
                if block == 0 or bit < low_bit(block):
                    sent[block + bit, chunk].wait_recv()
                    total = total + came[block + bit - 1, rows(chunk)].astype(F32)
            return total

        for block in firsts:
            for chunk in range(chunks):
                send(view(block + 1, chunk), block + 1, chunk, 1)
                loads[block, chunk] = local_copy(
                    view(block, chunk),
                    held.at[block // 2, rows(chunk)],
                    r[self.load].at[block // 2, chunk],
                )
        start, middle, pace, last = clock
        yield start
        for block in firsts:
            if block:
                for chunk in range(chunks):
                    if low_bit(block) > 2:
                        yield middle + chunk * pace
                    held[block // 2, rows(chunk)] = summed(block, chunk).astype(BF16)
                    send(held.at[block // 2, rows(chunk)], block, chunk, low_bit(block))
        for chunk in range(chunks):
            yield last + chunk * pace
            finish(chunk, summed(0, chunk))
        for copy in sent.values():
            copy.wait_send()


def norm_back_parts(value, gain, gradient):
    xh, rate = norm_parts(value)
    mg = gradient * gain
    back = rate * (
        mg - jnp.mean(mg, axis=-1, keepdims=True) - xh * jnp.mean(mg * xh, axis=-1, keepdims=True)
    )
    return back, jnp.sum(gradient * xh, axis=0, keepdims=True), jnp.sum(gradient, axis=0, keepdims=True)


def stream_flow(
    value=None,
    gain=None,
    shift=None,
    terms=None,
    above=None,
    rs=1,
    ag=1,
    keep=True,
    late=None,
    everyone=(),
    clock=(5, 30, 6, 60),
    gather_clock=(30, 6),
):
    if value is None:
        tokens, model = terms.shape[0] // rs, terms.shape[1]
    else:
        tokens, model = value.shape
    ag_bits = bits_of(ag)
    chunks = 4 if tokens % 64 == 0 else 1
    part = tokens // chunks
    flow = Flow([(TENSOR, bit) for bit in bits_of(max(rs, ag))] + list(everyone))
    if value is not None:
        value_key = flow.take(value, VMEM)
        gain_key = flow.take(gain[None], VMEM)
    if shift is not None:
        shift_key = flow.take(shift[None], VMEM)
    if above is not None:
        above_key = flow.take(above, VMEM)
        gain_sum = flow.give((1, model), F32, VMEM)
        shift_sum = flow.give((1, model), F32, VMEM)
    if rs > 1:
        terms_key = flow.take(terms)
        total_of = Sum(flow, rs, chunks, tokens, model)
    if keep:
        stream_key = flow.give((tokens, model), F32, VMEM)
    result_key = flow.give((ag * tokens, model), BF16, HBM if ag > 1 else VMEM)
    if ag > 1:
        own_key = flow.vmem(tokens, model)
        keep_sem = flow.sems(chunks)
        ag_send = flow.sems(ag, chunks)
        ag_recv = flow.sems(ag, chunks)
    if late is not None:
        late_key = flow.take(late, VMEM)
        all_key = flow.give((8, model), F32, VMEM)
        totals_key = flow.vmem(len(everyone) + 1, 8, model, dtype=F32)
        others_key = flow.vmem(len(everyone), 8, model, dtype=F32)
        totals_send = flow.sems(len(everyone))
        totals_recv = flow.sems(len(everyone))

    def rows(chunk):
        return pl.ds(chunk * part, part)

    def steps(r):
        t = lax.axis_index(TENSOR)

        def at(block, group, chunk):
            start = (peer(t, block) % group) * tokens + chunk * part
            return pl.ds(pl.multiple_of(start, 16), part)

        sent, keeps = {}, []

        def send(src, dst, block, chunk, bit):
            sent[block, chunk] = remote(
                src,
                dst,
                r[ag_send].at[block, chunk],
                r[ag_recv].at[block, chunk],
                TENSOR,
                partner(t, bit),
            )

        def finish(chunk, total):
            here = rows(chunk)
            if value is None:
                r[result_key][here, :] = total.astype(BF16)
                return
            stream = r[value_key][here, :].astype(F32)
            if above is None:
                if total is not None:
                    stream = stream + total
                    r[stream_key][here, :] = stream
                xh, unused = norm_parts(stream)
                result = (xh * r[gain_key][...] + r[shift_key][...]).astype(BF16)
            else:
                back, gains, shifts = norm_back_parts(stream, r[gain_key][...], total)
                if chunk == 0:
                    r[gain_sum][...] = gains
                    r[shift_sum][...] = shifts
                else:
                    r[gain_sum][...] += gains
                    r[shift_sum][...] += shifts
                gradient = r[above_key][here, :].astype(F32) + back
                if keep:
                    r[stream_key][here, :] = gradient
                result = gradient.astype(BF16)
            if ag == 1:
                r[result_key][here, :] = result
                return
            r[own_key][here, :] = result
            place = r[result_key].at[at(0, ag, chunk)]
            keeps.append(local_copy(r[own_key].at[here], place, r[keep_sem].at[chunk]))
            for bit in reversed(ag_bits):
                send(r[own_key].at[here], place, bit, chunk, bit)

        if rs > 1:
            yield from total_of.steps(
                r,
                lambda block, chunk: r[terms_key].at[at(block, rs, chunk)],
                rows,
                finish,
                clock,
            )
        else:
            for chunk in range(chunks):
                finish(chunk, None)
        if late is not None:
            count = late.shape[0]
            totals, others = r[totals_key], r[others_key]
            totals[0, :count] = r[late_key][...]
            totals[0, count : count + 1] = r[gain_sum][...]
            totals[0, count + 1 : count + 2] = r[shift_sum][...]
            totals[0, count + 2 :] = jnp.zeros_like(totals[0, count + 2 :])
            for i, (axis, bit) in enumerate(everyone):
                copy = remote(
                    totals.at[i],
                    others.at[i],
                    r[totals_send].at[i],
                    r[totals_recv].at[i],
                    axis,
                    partner(lax.axis_index(axis), bit),
                )
                yield clock[-1] + 40 + 15 * i
                copy.wait()
                totals[i + 1] = totals[i] + others[i]
            r[all_key][...] = totals[len(everyone)]
        first, pace = gather_clock
        for i, block in enumerate(sorted(range(2, ag, 2), key=lambda b: (level_of(b), low_bit(b)))):
            for chunk in range(chunks):
                yield first + (i * chunks + chunk) * pace
                sent[block, chunk].wait_recv()
                for bit in reversed(ag_bits):
                    if bit < low_bit(block):
                        place = r[result_key].at[at(block, ag, chunk)]
                        send(place, place, block + bit, chunk, bit)
        for (block, chunk), copy in sent.items():
            copy.wait_send()
            if block % 2:
                copy.wait_recv()
        for copy in keeps:
            copy.wait()

    flow.steps = steps
    return flow


def spread_on(side, block, bit):
    if block == 0:
        return True
    return bit < low_bit(block) if side == 0 else bit > high_bit(block)


def fetch_flow(weights, half, n_dp, window=3, clock=(8, 6.5)):
    dp_bits = bits_of(n_dp)
    units = [
        (which, plane, side)
        for which, (by_rows, weight) in enumerate(weights)
        for plane in range(weight.shape[0])
        for side in range(2)
    ]
    flow = Flow([(TENSOR, half)] + [(DP, bit) for bit in dp_bits])
    sources, targets, owns = [], [], []
    for by_rows, weight in weights:
        planes, high, wide = weight.shape
        sources.append(flow.take(weight))
        both = (planes, 2 * high, wide) if by_rows else (planes, high, 2 * wide)
        targets.append(flow.give(both, BF16))
        owns.append(flow.vmem(*weight.shape))
    sends = flow.sems(len(units), n_dp)
    recvs = flow.sems(len(units), n_dp)
    takes = flow.sems(len(weights))
    keep_sems = flow.sems(len(weights))

    def steps(r):
        t = lax.axis_index(TENSOR)
        d = lax.axis_index(DP)
        copies, keeps = {}, []

        def places(unit, block):
            which, plane, side = unit
            by_rows, weight = weights[which]
            source, target = r[sources[which]], r[targets[which]]
            high, wide = weight.shape[1:]
            size = (wide if by_rows else high) // n_dp // 2
            start = (peer(d, block) * 2 + side) * size
            if by_rows:
                columns = pl.ds(pl.multiple_of(start, 128), size)
                return source.at[plane, :, columns], target.at[plane, pl.ds(high, high), columns]
            rows = pl.ds(pl.multiple_of(start, 16), size)
            return source.at[plane, rows], target.at[plane, rows, pl.ds(wide, wide)]

        def send(src, dst, unit, block, axis, index):
            copies[unit, block] = remote(
                src, dst, r[sends].at[unit, block], r[recvs].at[unit, block], axis, index
            )

        def begin(unit):
            if unit < len(units):
                src, dst = places(units[unit], 0)
                send(src, dst, unit, 0, TENSOR, partner(t, half))

        def forward(unit, block):
            copies[unit, block].wait_recv()
            place = places(units[unit], block)[1]
            for bit in dp_bits:
                if spread_on(units[unit][2], block, bit):
                    send(place, place, unit, block + bit, DP, partner(d, bit))

        for unit in range(window):
            begin(unit)
        for which in range(len(weights)):
            keeps.append(local_copy(r[sources[which]], r[owns[which]], r[takes].at[which]))
        yield clock[0]
        for which, (by_rows, weight) in enumerate(weights):
            high, wide = weight.shape[1:]
            target = r[targets[which]]
            target = target.at[:, pl.ds(0, high)] if by_rows else target.at[:, :, pl.ds(0, wide)]
            keeps[which].wait()
            keeps[which] = local_copy(r[owns[which]], target, r[keep_sems].at[which])
        for step in range(len(units) + len(dp_bits) - 1):
            if step < len(units):
                forward(step, 0)
                begin(step + window)
            for level in range(1, len(dp_bits)):
                if 0 <= step - level < len(units):
                    for block in range(1, n_dp):
                        if level_of(block) == level:
                            forward(step - level, block)
            yield clock[0] + (step + 1) * clock[1]
        for unit in range(len(units)):
            copies[unit, n_dp - 1].wait_recv()
        for copy in copies.values():
            copy.wait_send()
        for copy in keeps:
            copy.wait()

    flow.steps = steps
    return flow


def text_flow(text, half, n, clock=(20, 12)):
    high, wide = text.shape[0] // (n // half), text.shape[1]
    flow = Flow([(TENSOR, bit) for bit in bits_of(n)])
    text_key = flow.take(text)
    result_key = flow.give((high, wide * n), BF16)
    own_key = flow.vmem(high, wide)
    sends, recvs, keeps = flow.sems(n), flow.sems(n), flow.sems(2)

    def steps(r):
        t = lax.axis_index(TENSOR)
        row = t // half
        copies = {}

        def rows(which):
            return r[text_key].at[pl.ds(pl.multiple_of(which * high, 16), high)]

        def columns(block):
            return r[result_key].at[:, pl.ds(pl.multiple_of(peer(t, block) * wide, 128), wide)]

        def send(src, dst, block, bit):
            copies[block] = remote(
                src, dst, r[sends].at[block], r[recvs].at[block], TENSOR, partner(t, bit)
            )

        for bit in reversed(bits_of(n)):
            send(rows(1 - row if bit == half else row), columns(0), bit, bit)
        keep = local_copy(rows(row), r[own_key], r[keeps].at[0])
        yield clock[0]
        keep.wait()
        keep = local_copy(r[own_key], columns(0), r[keeps].at[1])
        for i, block in enumerate(sorted(range(1, n), key=lambda b: (level_of(b), low_bit(b)))):
            copies[block].wait_recv()
            for bit in reversed(bits_of(n)):
                if bit < low_bit(block):
                    send(columns(block), columns(block), block + bit, bit)
            yield clock[0] + i * clock[1]
        for copy in copies.values():
            copy.wait_send()
        keep.wait()

    flow.steps = steps
    return flow


def text_back_flow(terms, half, n, clocks=((8, 30, 6, 30), (9, 30, 6, 35), 45)):
    high, wide = terms.shape[0], terms.shape[1] // n
    flow = Flow([(TENSOR, bit) for bit in bits_of(n)])
    terms_key = flow.take(terms)
    result_key = flow.give((high * (n // half), wide), BF16)
    sums = [Sum(flow, half, 1, high, wide) for unused in range(2)]
    owns = [flow.vmem(high, wide) for unused in range(2)]
    sems = flow.sems(3)

    def steps(r):
        t = lax.axis_index(TENSOR)
        row = t // half
        last = []

        def view(far):
            def place(block, chunk):
                column = peer(t, block + far) * wide
                return r[terms_key].at[:, pl.ds(pl.multiple_of(column, 128), wide)]

            return place

        def target():
            return r[result_key].at[pl.ds(pl.multiple_of(row * high, 16), high)]

        def finish_far(chunk, total):
            r[owns[0]][...] = total.astype(BF16)
            last.append(
                remote(
                    r[owns[0]],
                    target(),
                    r[sems].at[0],
                    r[sems].at[1],
                    TENSOR,
                    partner(t, half),
                )
            )

        def finish_near(chunk, total):
            r[owns[1]][...] = total.astype(BF16)
            last.append(local_copy(r[owns[1]], target(), r[sems].at[2]))

        def rows(chunk):
            return pl.ds(0, high)

        parts = [
            [0, sums[0].steps(r, view(half), rows, finish_far, clocks[0])],
            [0, sums[1].steps(r, view(0), rows, finish_near, clocks[1])],
        ]
        while parts:
            entry = min(parts, key=lambda e: e[0])
            if entry[0]:
                yield entry[0]
            moment = next(entry[1], None)
            if moment is None:
                parts.remove(entry)
            else:
                entry[0] = moment
        yield clocks[2]
        for copy in last:
            copy.wait()

    flow.steps = steps
    return flow


def grads_flow(grads, n_dp, outs, half=0, summing=True, window=4, clock=(10, 20), slack=1):
    high, whole = grads[0].shape[1:]
    high = high if summing else high * n_dp
    wide = whole // 2 if half else whole
    size = high // n_dp // 2
    dp_bits = bits_of(n_dp)
    units = [
        (which, plane, side)
        for which, grad in enumerate(grads)
        for plane in range(grad.shape[0])
        for side in range(2)
    ]
    count = len(units)
    depth = len(dp_bits)
    slots = n_dp // 2 if summing else 1
    flow = Flow([(DP, bit) for bit in dp_bits] + ([(TENSOR, half)] if half else []))
    sources = [flow.take(grad) for grad in grads]
    targets = [flow.give((n, high, wide) if n else (wide, high), BF16) for n in outs]
    target_of = [(i, plane) for i, n in enumerate(outs) for plane in range(max(n, 1))]
    flat = [(grad, plane) for grad in range(len(grads)) for plane in range(grads[grad].shape[0])]
    gathered = flow.vmem(len(flat), high, wide)
    turned = [unit for unit in range(count) if not outs[target_of[flat.index(units[unit][:2])][0]]]
    if turned:
        staged = flow.vmem(len(turned), n_dp, wide, size)
    if summing:
        held = flow.vmem(count, slots, size, whole)
    load_sems = flow.sems(count, slots)
    if summing:
        came = flow.vmem(count, n_dp - 1, size, whole)
        sum_send, sum_recv = flow.sems(count, n_dp), flow.sems(count, n_dp)
    if half:
        given = flow.vmem(count, size, wide)
        mid_send, mid_recv = flow.sems(count), flow.sems(count)
        if summing:
            mine = flow.vmem(count, size, wide, dtype=F32)
            theirs = flow.vmem(count, size, wide)
    ag_send, ag_recv = flow.sems(count, n_dp), flow.sems(count, n_dp)
    keep_sems = flow.sems(count, n_dp)

    def order(side):
        return dp_bits if side == 0 else tuple(reversed(dp_bits))

    def stage(side, block):
        return min(i for i, bit in enumerate(order(side)) if block & bit)

    def slot(side, block):
        return [b for b in range(n_dp) if b == 0 or stage(side, b) > 0].index(block)

    def steps(r):
        d = lax.axis_index(DP)
        sums, loads, mids, spreads, keeps = {}, {}, {}, {}, []

        def rows_of(unit, block):
            return pl.ds(pl.multiple_of((peer(d, block) * 2 + units[unit][2]) * size, 16), size)

        def source_of(unit, block):
            which, plane, side = units[unit]
            rows = rows_of(unit, block) if summing else pl.ds(side * size, size)
            return r[sources[which]].at[plane, rows]

        def region(unit, block):
            return r[gathered].at[flat.index(units[unit][:2]), rows_of(unit, block)]

        def swap(src, unit):
            mids[unit] = remote(
                src,
                r[given].at[unit],
                r[mid_send].at[unit],
                r[mid_recv].at[unit],
                TENSOR,
                partner(lax.axis_index(TENSOR), half),
            )

        def send(src, unit, block):
            side = units[unit][2]
            sums[unit, block] = remote(
                src,
                r[came].at[unit, block - 1],
                r[sum_send].at[unit, block],
                r[sum_recv].at[unit, block],
                DP,
                partner(d, order(side)[stage(side, block)]),
            )

        def summed(unit, block):
            side = units[unit][2]
            loads[unit, block].wait()
            total = r[held][unit, slot(side, block)].astype(F32)
            for i, bit in enumerate(order(side)):
                if summing and (block == 0 or i < stage(side, block)):
                    sums[unit, block + bit].wait_recv()
                    total = total + r[came][unit, block + bit - 1].astype(F32)
            return total

        def begin(unit):
            if unit >= count:
                return
            side = units[unit][2]
            if not summing:
                source = source_of(unit, 0)
                swap(source.at[:, pl.ds(wide, wide)], unit)
                loads[unit, 0] = local_copy(
                    source.at[:, pl.ds(0, wide)], region(unit, 0), r[load_sems].at[unit, 0]
                )
                return
            for block in range(n_dp):
                source = source_of(unit, block)
                if block and stage(side, block) == 0:
                    send(source, unit, block)
                else:
                    place = slot(side, block)
                    loads[unit, block] = local_copy(
                        source, r[held].at[unit, place], r[load_sems].at[unit, place]
                    )

        def middle(unit, level):
            side = units[unit][2]
            for block in range(1, n_dp):
                if stage(side, block) == level:
                    r[held][unit, slot(side, block)] = summed(unit, block).astype(BF16)
                    send(r[held].at[unit, slot(side, block)], unit, block)

        def cross(unit):
            if half and summing:
                total = summed(unit, 0)
                r[mine][unit] = total[:, :wide]
                r[theirs][unit] = total[:, wide:].astype(BF16)
                swap(r[theirs].at[unit], unit)

        def spread(unit, block, src, dst):
            for bit in dp_bits:
                if spread_on(units[unit][2], block, bit):
                    spreads[unit, block + bit] = remote(
                        src,
                        dst,
                        r[ag_send].at[unit, block + bit],
                        r[ag_recv].at[unit, block + bit],
                        DP,
                        partner(d, bit),
                    )

        def settle(unit):
            place = region(unit, 0)
            if half and summing:
                total = r[mine][unit]
            elif summing:
                total = summed(unit, 0)
            else:
                loads[unit, 0].wait()
                total = place[...].astype(F32)
            if half:
                mids[unit].wait_recv()
                total = total + r[given][unit].astype(F32)
            place[...] = total.astype(BF16)
            spread(unit, 0, place, place)

        def onward(unit, level):
            for block in range(1, n_dp):
                if level_of(block) == level:
                    spreads[unit, block].wait_recv()
                    place = region(unit, block)
                    spread(unit, block, place, place)

        def write(unit):
            spreads[unit, n_dp - 1].wait_recv()
            which, plane = target_of[flat.index(units[unit][:2])]
            target = r[targets[which]]
            for block in range(n_dp):
                src = region(unit, block)
                if outs[which]:
                    to = target.at[plane, rows_of(unit, block)]
                else:
                    place = turned.index(unit)
                    r[staged][place, block] = src[...].astype(F32).T.astype(BF16)
                    src = r[staged].at[place, block]
                    start = (peer(d, block) * 2 + units[unit][2]) * size
                    to = target.at[:, pl.ds(pl.multiple_of(start, 128), size)]
                keeps.append(local_copy(src, to, r[keep_sems].at[unit, block]))

        for unit in range(window):
            begin(unit)
        start = max(depth - 1, 0) if summing else 0
        first = start + (1 if summing else 0) + (slack if half else 0)
        for step in range(count + first + depth):
            yield clock[0] + step * clock[1]

            def turn(lag, action, *more):
                if 0 <= step - lag < count:
                    action(step - lag, *more)

            turn(first + depth, write)

            for level in range(depth - 1, 0, -1):
                turn(first + level, onward, level)
            turn(first, settle)
            turn(start, cross)
            if summing:
                for level in range(depth - 1, 0, -1):
                    turn(level - 1, middle, level)
            begin(step + window)
        for copy in [*sums.values(), *mids.values(), *spreads.values()]:
            copy.wait_send()
        for copy in keeps:
            copy.wait()

    flow.steps = steps
    return flow


def dot_flow(left, right, turned=False, parts=8, clock=(4, 8)):
    flow = Flow([])
    high, deep = left.shape
    wide = right.shape[0] if turned else right.shape[1]
    part = high // parts
    left_key, right_key = flow.take(left), flow.take(right)
    result_key = flow.give((high, wide), BF16)
    lefts, rights = flow.vmem(2, part, deep), flow.vmem(*right.shape)
    results = flow.vmem(2, part, wide)
    sems, right_sem = flow.sems(2, 2), flow.sems(1)

    def steps(r):
        loads, stores = {}, {}

        def load(i):
            if i < parts:
                loads[i] = local_copy(
                    r[left_key].at[pl.ds(i * part, part)], r[lefts].at[i % 2], r[sems].at[0, i % 2]
                )

        whole = local_copy(r[right_key], r[rights], r[right_sem].at[0])
        load(0)
        load(1)
        for i in range(parts):
            yield clock[0] + i * clock[1]
            if i == 0:
                whole.wait()
            loads[i].wait()
            if i > 1:
                stores[i - 2].wait()
            dims = (((1,), (1 if turned else 0,)), ((), ()))
            value = lax.dot_general(
                r[lefts][i % 2], r[rights][...], dims, preferred_element_type=F32
            )
            r[results][i % 2] = value.astype(BF16)
            stores[i] = local_copy(
                r[results].at[i % 2], r[result_key].at[pl.ds(i * part, part)], r[sems].at[1, i % 2]
            )
            load(i + 2)
        for i in range(max(parts - 2, 0), parts):
            stores[i].wait()

    flow.steps = steps
    return flow


def pass_flow(value):
    flow = Flow([])
    value_key = flow.take(value)
    result_key = flow.give(value.shape, value.dtype)
    held = flow.vmem(*value.shape)
    sems = flow.sems(2)

    def steps(r):
        copy = local_copy(r[value_key], r[held], r[sems].at[0])
        yield 8
        copy.wait()
        copy = local_copy(r[held], r[result_key], r[sems].at[1])
        yield 30
        copy.wait()

    flow.steps = steps
    return flow


def nothing(*refs):
    pass


def after(value, *before):
    return pl.pallas_call(
        nothing,
        in_specs=[HBM] * (1 + len(before)),
        out_specs=HBM,
        out_shape=jax.ShapeDtypeStruct(value.shape, value.dtype),
        input_output_aliases={0: 0},
    )(value, *before)


def local(
    image,
    text,
    cotangent,
    norm_gains,
    norm_shifts,
    w_self,
    w_self_out,
    w_cross_q,
    w_cross_kv,
    w_cross_out,
    w_text,
    w_up,
    w_down,
    segment_ids,
    caption_lengths,
):
    rows_here = segment_ids.shape[0]
    n_tensor = lax.axis_size(TENSOR)
    n_dp = lax.axis_size(DP)
    half = n_tensor // rows_here
    row = lax.axis_index(TENSOR) // half
    width = w_self.shape[2]
    slots = IMGS * CAP

    seg = lax.dynamic_index_in_dim(segment_ids, row, 0, keepdims=False)
    seg_col = seg[:, None]
    seg_row = seg[None, :]
    lengths = lax.dynamic_index_in_dim(caption_lengths.reshape(rows_here, IMGS), row, 0, keepdims=False)
    slot = jnp.arange(slots, dtype=jnp.int32)
    live = (slot % CAP) < jnp.repeat(lengths, CAP)
    slot_row = jnp.where(live, slot // CAP, -1)[None, :]

    (w_self2, w_self_out2), (n1,), (later,), (text_columns,) = run_flows(
        0,
        "start",
        60,
        fetch_flow(((False, w_self), (True, w_self_out[None])), half, n_dp),
        stream_flow(
            image, norm_gains[0], norm_shifts[0], ag=half, keep=False, gather_clock=(12, 11)
        ),
        pass_flow(cotangent),
        dot_flow(text, w_text),
    )
    w_self_out2 = w_self_out2[0]
    triple = planes_of(n1, w_self2)
    o1 = attend(seg_col, seg_row, (triple, 0), (triple, 1), (triple, 2))
    p1 = dot(o1, w_self_out2).astype(BF16)
    e3 = lax.all_gather(later, TENSOR, axis=0, tiled=True)
    (x1, n2), (w_kv2, w_cross_q2, w_cross_out2), (projected,) = run_flows(
        1,
        "self_sum",
        100,
        stream_flow(
            image,
            norm_gains[1],
            norm_shifts[1],
            terms=p1,
            rs=half,
            ag=half,
            clock=(5, 0, 10, 18),
            gather_clock=(60, 10),
        ),
        fetch_flow(
            ((False, w_cross_kv), (False, w_cross_q[None]), (True, w_cross_out[None])),
            half,
            n_dp,
            clock=(20, 8),
        ),
        text_flow(text_columns, half, n_tensor),
    )
    w_cross_q2, w_cross_out2 = w_cross_q2[0], w_cross_out2[0]

    pair = planes_of(projected, w_kv2)
    q2 = dot(n2, w_cross_q2).astype(BF16)
    o2 = attend(seg_col, slot_row, (q2, None), (pair, 0), (pair, 1))
    p2 = dot(o2, w_cross_out2).astype(BF16)
    (x2, n3), (active_back,) = run_flows(
        2,
        "cross_sum",
        100,
        stream_flow(
            x1,
            norm_gains[2],
            norm_shifts[2],
            terms=p2,
            rs=half,
            ag=n_tensor,
            clock=(5, 0, 6, 15),
            gather_clock=(40, 6),
        ),
        dot_flow(e3, w_down, True, clock=(4, 11)),
    )

    act, dh = hidden_step(n3, w_up, active_back)
    down_grad = dot_t(act, e3).astype(BF16)
    up_grad = dot_t(n3, dh).astype(BF16)
    sums = lax.psum((down_grad, up_grad), DP)
    p3 = after(rows_dot([dh], w_up[None]), down_grad, up_grad)
    (gain_two, shift_two, g2, e2), (p6,) = run_flows(
        3,
        "up_sum",
        100,
        stream_flow(
            x2, norm_gains[2], terms=p3, above=cotangent, rs=n_tensor, ag=half, clock=(8, 30, 6, 60)
        ),
        dot_flow(act, w_down, clock=(12, 10)),
    )

    do2 = dot_r(e2, w_cross_out2).astype(BF16)
    dq2, dk2, dv2 = attend_back(seg_col, slot_row, (q2, None), (pair, 0), (pair, 1), do2)
    p4 = rows_dot([dq2], w_cross_q2[None])
    pair_back = jnp.stack([dk2, dv2])
    cross = jnp.concatenate(
        [
            dot_t(n2, dq2).astype(BF16)[None],
            planes_grad(projected, pair_back),
            dot_t(e2, o2).astype(BF16)[None],
        ]
    )
    cross_part = lax.psum_scatter(cross, DP, scatter_dimension=1, tiled=True)
    dproj = rows_dot([dk2, dv2], w_kv2)
    (gain_one, shift_one, g1, e1), (dproj,) = run_flows(
        4,
        "query_sum",
        60,
        stream_flow(
            x1,
            norm_gains[1],
            terms=after(p4, cross),
            above=g2,
            rs=half,
            ag=half,
            clock=(5, 0, 6, 15),
            gather_clock=(37, 6),
        ),
        text_back_flow(dproj, half, n_tensor),
    )

    down_sum = lax.psum_scatter(after(p6, e1), TENSOR, scatter_dimension=0, tiled=True)
    image_out = (x2 + down_sum.astype(F32)).astype(BF16)

    do1 = dot_r(e1, w_self_out2).astype(BF16)
    dq1, dk1, dv1 = attend_back(seg_col, seg_row, (triple, 0), (triple, 1), (triple, 2), do1)
    triple_back = jnp.stack([dq1, dk1, dv1])
    own = planes_grad(n1, triple_back)
    own_out = dot_t(e1, o1).astype(BF16)[None]
    p5 = planes_back(triple_back, w_self2)
    text_w_part = columns_dot(text, dproj)
    p7 = rows_dot([dproj], w_text[None], 1024)
    text_grad = lax.psum_scatter(p7, TENSOR, scatter_dimension=0, tiled=True)
    everyone = [(TENSOR, bit) for bit in bits_of(n_tensor)] + [(DP, bit) for bit in bits_of(n_dp)]
    late = jnp.concatenate([gain_one, shift_one, gain_two, shift_two])
    (
        (self_grad, self_out_grad),
        (unused, unused, image_grad, all_sums),
        (cross_q_grad, cross_kv_grad, cross_out_grad),
        (text_w_grad,),
    ) = run_flows(
        5,
        "end",
        200,
        grads_flow((own, own_out), n_dp, (3, 0), half, clock=(14, 14)),
        stream_flow(
            image,
            norm_gains[0],
            terms=p5,
            above=g1,
            rs=half,
            keep=False,
            late=late,
            everyone=everyone,
            clock=(6, 0, 8, 50),
        ),
        grads_flow((cross_part,), n_dp, (1, 2, 0), half, summing=False, clock=(15, 12)),
        grads_flow((text_w_part.reshape(4, -1, width),), n_dp, (4,), clock=(10, 16)),
    )
    down_grad, up_grad = [value.astype(F32) for value in sums]
    self_grad, self_out_grad = self_grad.astype(F32), self_out_grad.astype(F32)
    cross_q_grad, cross_kv_grad = cross_q_grad[0].astype(F32), cross_kv_grad.astype(F32)
    cross_out_grad = cross_out_grad.astype(F32)
    text_w_grad = text_w_grad.reshape(-1, width).astype(F32)
    gain_grad = jnp.stack([all_sums[4], all_sums[0], all_sums[2]])
    shift_grad = jnp.stack([all_sums[5], all_sums[1], all_sums[3]])
    return (
        image_out,
        image_grad,
        text_grad,
        gain_grad,
        shift_grad,
        self_grad,
        self_out_grad,
        cross_q_grad,
        cross_kv_grad,
        cross_out_grad,
        text_w_grad,
        up_grad,
        down_grad,
    )


def solution(mesh):
    tokens = P((DP, TENSOR), None)
    columns = P(None, TENSOR)
    planes = P(None, None, TENSOR)
    rows = P(TENSOR, None)
    return jax.shard_map(
        local,
        mesh=mesh,
        in_specs=(
            tokens,
            P(DP, None),
            tokens,
            P(),
            P(),
            planes,
            rows,
            columns,
            planes,
            rows,
            columns,
            columns,
            rows,
            P(DP, None),
            P(DP),
        ),
        out_specs=(
            tokens,
            tokens,
            tokens,
            P(),
            P(),
            planes,
            rows,
            columns,
            planes,
            rows,
            columns,
            columns,
            rows,
        ),
        check_vma=False,
    )
```

```python
import functools

import jax
import jax.numpy as jnp
from jax import lax
from jax.experimental import pallas as pl
from jax.experimental.pallas import tpu as pltpu
from jax.sharding import PartitionSpec as P

HD = 128
IMGS = 4
CAP = 128
SCALE = HD ** (-0.5)
LOG2E = 1.4426950408889634
MIB = 1024 * 1024

epsilon = 1e-05
masked_value = -1e30

TENSOR = "tensor"
DP = "dp"

F32 = jnp.float32
BF16 = jnp.bfloat16


def raised_of(q, k, allowed):
    raw = lax.dot_general(q, k, (((1,), (1,)), ((), ())), preferred_element_type=F32)
    scores = jnp.where(allowed, raw * (SCALE * LOG2E), masked_value)
    raised = jnp.exp2(scores - jnp.max(scores, axis=-1, keepdims=True))
    return raised, 1.0 / jnp.sum(raised, axis=-1, keepdims=True)


def attend_kernel(step, qid_ref, kid_ref, q_ref, k_ref, v_ref, o_ref):
    k = k_ref[...]
    v = v_ref[...]
    kid = kid_ref[...]
    for start in range(0, q_ref.shape[0], step):
        rows = pl.ds(start, step)
        raised, rate = raised_of(q_ref[rows, :], k, qid_ref[rows, :] == kid)
        mixed = jnp.dot(raised.astype(BF16), v, preferred_element_type=F32)
        o_ref[rows, :] = (mixed * rate).astype(BF16)


def attend_back_kernel(step, qid_ref, kid_ref, q_ref, k_ref, v_ref, do_ref, dq_ref, dk_ref, dv_ref, dk_sum, dv_sum):
    k = k_ref[...]
    v = v_ref[...]
    kid = kid_ref[...]
    for start in range(0, q_ref.shape[0], step):
        rows = pl.ds(start, step)
        q = q_ref[rows, :]
        do = do_ref[rows, :]
        raised, rate = raised_of(q, k, qid_ref[rows, :] == kid)
        dp = lax.dot_general(do, v, (((1,), (1,)), ((), ())), preferred_element_type=F32)
        inner = jnp.sum(dp * raised, axis=-1, keepdims=True) * rate
        ds = (raised * ((dp - inner) * (rate * SCALE))).astype(BF16)
        dq_ref[rows, :] = jnp.dot(ds, k, preferred_element_type=F32).astype(BF16)
        dk = lax.dot_general(ds, q, (((0,), (0,)), ((), ())), preferred_element_type=F32)
        shared = (do.astype(F32) * rate).astype(BF16)
        dv = lax.dot_general(
            raised.astype(BF16), shared, (((0,), (0,)), ((), ())), preferred_element_type=F32
        )
        if start == 0:
            dk_sum[...] = dk
            dv_sum[...] = dv
        else:
            dk_sum[...] += dk
            dv_sum[...] += dv
    dk_ref[...] = dk_sum[...].astype(BF16)
    dv_ref[...] = dv_sum[...].astype(BF16)


def head_spec(rows, which):
    if which is None:
        return pl.BlockSpec((rows, HD), lambda h: (0, h))
    return pl.BlockSpec((None, rows, HD), lambda h: (which, 0, h))


def whole_spec(shape):
    return pl.BlockSpec(shape, lambda h: (0, 0))


def attend(qid, kid, query, keys, values):
    (qa, qp), (ka, kp), (va, vp) = query, keys, values
    tokens, width = qa.shape[-2:]
    slots = ka.shape[-2]
    heads = width // HD
    return pl.pallas_call(
        functools.partial(attend_kernel, 256),
        grid=(heads,),
        in_specs=[
            whole_spec(qid.shape),
            whole_spec(kid.shape),
            head_spec(tokens, qp),
            head_spec(slots, kp),
            head_spec(slots, vp),
        ],
        out_specs=head_spec(tokens, None),
        out_shape=jax.ShapeDtypeStruct((tokens, width), BF16),
        compiler_params=pltpu.CompilerParams(vmem_limit_bytes=48 * MIB),
        cost_estimate=pl.CostEstimate(
            flops=4 * tokens * slots * width,
            bytes_accessed=2 * width * (2 * tokens + 2 * slots),
            transcendentals=tokens * slots * heads,
        ),
        name="attend",
    )(qid, kid, qa, ka, va)


def attend_back(qid, kid, query, keys, values, do):
    (qa, qp), (ka, kp), (va, vp) = query, keys, values
    tokens, width = qa.shape[-2:]
    slots = ka.shape[-2]
    heads = width // HD
    return pl.pallas_call(
        functools.partial(attend_back_kernel, 256),
        grid=(heads,),
        in_specs=[
            whole_spec(qid.shape),
            whole_spec(kid.shape),
            head_spec(tokens, qp),
            head_spec(slots, kp),
            head_spec(slots, vp),
            head_spec(tokens, None),
        ],
        out_specs=[head_spec(tokens, None), head_spec(slots, None), head_spec(slots, None)],
        out_shape=[
            jax.ShapeDtypeStruct((tokens, width), BF16),
            jax.ShapeDtypeStruct((slots, width), BF16),
            jax.ShapeDtypeStruct((slots, width), BF16),
        ],
        scratch_shapes=[pltpu.VMEM((slots, HD), F32), pltpu.VMEM((slots, HD), F32)],
        compiler_params=pltpu.CompilerParams(vmem_limit_bytes=48 * MIB),
        cost_estimate=pl.CostEstimate(
            flops=10 * tokens * slots * width,
            bytes_accessed=2 * width * (3 * tokens + 4 * slots),
            transcendentals=tokens * slots * heads,
        ),
        name="attend_back",
    )(qid, kid, qa, ka, va, do)


def dot(left, right):
    return jnp.dot(left, right, preferred_element_type=F32)


def dot_t(left, right):
    return lax.dot_general(left, right, (((0,), (0,)), ((), ())), preferred_element_type=F32)


def dot_r(left, right):
    return lax.dot_general(left, right, (((1,), (1,)), ((), ())), preferred_element_type=F32)


def rows_dot_kernel(count, *refs):
    total = None
    for left_ref, right_ref in zip(refs[:count], refs[count : 2 * count]):
        term = lax.dot_general(
            left_ref[...], right_ref[...], (((1,), (1,)), ((), ())), preferred_element_type=F32
        )
        total = term if total is None else total + term
    refs[-1][...] = total.astype(BF16)


def rows_dot(lefts, right, tile=512):
    count = len(lefts)
    high, deep = lefts[0].shape
    wide = right.shape[1]
    return pl.pallas_call(
        functools.partial(rows_dot_kernel, count),
        grid=(wide // tile,),
        in_specs=[pl.BlockSpec((high, deep), lambda n: (0, 0))] * count
        + [pl.BlockSpec((None, tile, deep), lambda n, c=c: (c, n, 0)) for c in range(count)],
        out_specs=pl.BlockSpec((high, tile), lambda n: (0, n)),
        out_shape=jax.ShapeDtypeStruct((high, wide), BF16),
        compiler_params=pltpu.CompilerParams(vmem_limit_bytes=48 * MIB),
        cost_estimate=pl.CostEstimate(
            flops=2 * count * high * deep * wide,
            bytes_accessed=2 * (count * deep * (high + wide) + high * wide),
            transcendentals=0,
        ),
        name="rows_dot",
    )(*lefts, *[right] * count)


def columns_dot_kernel(left_ref, right_ref, out_ref):
    out_ref[...] = lax.dot_general(
        left_ref[...], right_ref[...], (((0,), (0,)), ((), ())), preferred_element_type=F32
    ).astype(BF16)


def columns_dot(left, right, tile=512):
    deep, high = left.shape
    wide = right.shape[1]
    return pl.pallas_call(
        columns_dot_kernel,
        grid=(high // tile,),
        in_specs=[
            pl.BlockSpec((deep, tile), lambda n: (0, n)),
            pl.BlockSpec((deep, wide), lambda n: (0, 0)),
        ],
        out_specs=pl.BlockSpec((tile, wide), lambda n: (n, 0)),
        out_shape=jax.ShapeDtypeStruct((high, wide), BF16),
        compiler_params=pltpu.CompilerParams(vmem_limit_bytes=48 * MIB),
        cost_estimate=pl.CostEstimate(
            flops=2 * deep * high * wide,
            bytes_accessed=2 * (deep * (high + wide) + high * wide),
            transcendentals=0,
        ),
        name="columns_dot",
    )(left, right)


def planes_of(left, right):
    return jnp.einsum("td,cde->cte", left, right, preferred_element_type=F32).astype(BF16)


def planes_grad(left, right):
    return jnp.einsum("td,cta->cda", left, right, preferred_element_type=F32).astype(BF16)


def planes_back(left, right):
    return jnp.einsum("cta,cda->td", left, right, preferred_element_type=F32).astype(BF16)


def norm_parts(value):
    mean = jnp.mean(value, axis=-1, keepdims=True)
    centered = value - mean
    spread = jnp.mean(centered * centered, axis=-1, keepdims=True)
    rate = lax.rsqrt(spread + epsilon)
    return centered * rate, rate


def gelu_parts(h):
    c = 0.7978845608028654
    inner = c * (h + 0.044715 * h * h * h)
    th = jnp.tanh(inner)
    half = 0.5 * (1.0 + th)
    slope = half + 0.5 * h * (1.0 - th * th) * (c * (1.0 + 3 * 0.044715 * h * h))
    return h * half, slope


def hidden_kernel(tokens_ref, weight_ref, back_ref, act_ref, out_ref):
    h = jnp.dot(tokens_ref[...], weight_ref[...], preferred_element_type=F32)
    act, slope = gelu_parts(h)
    act_ref[...] = act.astype(BF16)
    out_ref[...] = (back_ref[...].astype(F32) * slope).astype(BF16)


def hidden_step(tokens, weight, back, tile=256):
    high, deep = tokens.shape
    wide = weight.shape[1]
    part = pl.BlockSpec((tile, wide), lambda m: (m, 0))
    return pl.pallas_call(
        hidden_kernel,
        grid=(high // tile,),
        in_specs=[
            pl.BlockSpec((tile, deep), lambda m: (m, 0)),
            pl.BlockSpec((deep, wide), lambda m: (0, 0)),
            part,
        ],
        out_specs=[part, part],
        out_shape=[jax.ShapeDtypeStruct((high, wide), BF16)] * 2,
        compiler_params=pltpu.CompilerParams(vmem_limit_bytes=48 * MIB),
        cost_estimate=pl.CostEstimate(
            flops=2 * high * deep * wide,
            bytes_accessed=2 * (high * deep + deep * wide + 3 * high * wide),
            transcendentals=high * wide,
        ),
        name="hidden_step",
    )(tokens, weight, back)


def partner(index, bit):
    return index + bit - 2 * bit * ((index // bit) % 2)


def peer(index, mask):
    bit = 1
    while bit <= mask:
        if mask & bit:
            index = partner(index, bit)
        bit *= 2
    return index


def low_bit(value):
    return value & -value


def high_bit(value):
    return 1 << (value.bit_length() - 1)


def level_of(value):
    return sum((value >> i) & 1 for i in range(value.bit_length()))


def bits_of(size):
    return tuple(1 << i for i in range(size.bit_length() - 1))


def remote(src, dst, send_sem, recv_sem, axis, index):
    copy = pltpu.make_async_remote_copy(
        src_ref=src,
        dst_ref=dst,
        send_sem=send_sem,
        recv_sem=recv_sem,
        device_id={axis: index},
        device_id_type=pl.DeviceIdType.MESH,
    )
    copy.start()
    return copy


def local_copy(src, dst, sem):
    copy = pltpu.make_async_copy(src, dst, sem)
    copy.start()
    return copy


VMEM = pl.BlockSpec(memory_space=pltpu.VMEM)
HBM = pl.BlockSpec(memory_space=pl.ANY)
DMA = pltpu.SemaphoreType.DMA


class Flow:
    def __init__(self, partners):
        self.partners = partners
        self.ins, self.outs, self.scratch = [], [], []
        self.steps = None

    def take(self, array, spec=HBM):
        self.ins.append((array, spec))
        return (0, len(self.ins) - 1)

    def give(self, shape, dtype, spec=HBM):
        self.outs.append((jax.ShapeDtypeStruct(shape, dtype), spec))
        return (1, len(self.outs) - 1)

    def hold(self, kind):
        self.scratch.append((kind, None))
        return (2, len(self.scratch) - 1)

    def vmem(self, *shape, dtype=BF16):
        return self.hold(pltpu.VMEM(shape, dtype))

    def sems(self, *shape):
        return self.hold(DMA(shape))


def flows_kernel(flows, *refs):
    refs = list(refs)
    tables = [{} for unused in flows]
    for part in range(3):
        for flow, table in zip(flows, tables):
            for i in range(len((flow.ins, flow.outs, flow.scratch)[part])):
                table[part, i] = refs.pop(0)
    partners = []
    for flow in flows:
        partners += [entry for entry in flow.partners if entry not in partners]
    barrier = pltpu.get_barrier_semaphore()
    for axis, bit in partners:
        pl.semaphore_signal(
            barrier,
            inc=1,
            device_id={axis: partner(lax.axis_index(axis), bit)},
            device_id_type=pl.DeviceIdType.MESH,
        )
    pl.semaphore_wait(barrier, len(partners))
    running = [[0.0, flow.steps(table)] for flow, table in zip(flows, tables)]
    while running:
        entry = min(running, key=lambda e: e[0])
        moment = next(entry[1], None)
        if moment is None:
            running.remove(entry)
        else:
            entry[0] = moment


def run_flows(cid, name, micros, *flows):
    ins, outs, scratch = [
        [entry for flow in flows for entry in part(flow)]
        for part in (lambda f: f.ins, lambda f: f.outs, lambda f: f.scratch)
    ]
    results = pl.pallas_call(
        functools.partial(flows_kernel, flows),
        in_specs=[entry[1] for entry in ins],
        out_specs=[entry[1] for entry in outs],
        out_shape=[entry[0] for entry in outs],
        scratch_shapes=[entry[0] for entry in scratch],
        compiler_params=pltpu.CompilerParams(
            collective_id=cid, has_side_effects=True, vmem_limit_bytes=58 * MIB
        ),
        cost_estimate=pl.CostEstimate(
            flops=0, bytes_accessed=int(micros * 3.3e6), transcendentals=0
        ),
        name=name,
    )(*[entry[0] for entry in ins])
    results = list(results)
    return [tuple(results.pop(0) for unused in flow.outs) for flow in flows]


class Sum:
    def __init__(self, flow, size, chunks, high, wide):
        self.size, self.chunks = size, chunks
        self.held = flow.vmem(size // 2, high, wide)
        self.came = flow.vmem(size - 1, high, wide)
        self.load = flow.sems(size // 2, chunks)
        self.sent = flow.sems(size, chunks)
        self.got = flow.sems(size, chunks)

    def steps(self, r, view, rows, finish, clock):
        bits = bits_of(self.size)
        chunks = self.chunks
        index = lax.axis_index(TENSOR)
        held, came = r[self.held], r[self.came]
        firsts = sorted(range(0, self.size, 2), reverse=True)
        sent, loads = {}, {}

        def send(src, block, chunk, bit):
            sent[block, chunk] = remote(
                src,
                came.at[block - 1, rows(chunk)],
                r[self.sent].at[block, chunk],
                r[self.got].at[block, chunk],
                TENSOR,
                partner(index, bit),
            )

        def summed(block, chunk):
            loads[block, chunk].wait()
            total = held[block // 2, rows(chunk)].astype(F32)
            for bit in bits:
                if block == 0 or bit < low_bit(block):
                    sent[block + bit, chunk].wait_recv()
                    total = total + came[block + bit - 1, rows(chunk)].astype(F32)
            return total

        for block in firsts:
            for chunk in range(chunks):
                send(view(block + 1, chunk), block + 1, chunk, 1)
                loads[block, chunk] = local_copy(
                    view(block, chunk),
                    held.at[block // 2, rows(chunk)],
                    r[self.load].at[block // 2, chunk],
                )
        start, middle, pace, last = clock
        yield start
        for block in firsts:
            if block:
                for chunk in range(chunks):
                    if low_bit(block) > 2:
                        yield middle + chunk * pace
                    held[block // 2, rows(chunk)] = summed(block, chunk).astype(BF16)
                    send(held.at[block // 2, rows(chunk)], block, chunk, low_bit(block))
        for chunk in range(chunks):
            yield last + chunk * pace
            finish(chunk, summed(0, chunk))
        for copy in sent.values():
            copy.wait_send()


def norm_back_parts(value, gain, gradient):
    xh, rate = norm_parts(value)
    mg = gradient * gain
    back = rate * (
        mg - jnp.mean(mg, axis=-1, keepdims=True) - xh * jnp.mean(mg * xh, axis=-1, keepdims=True)
    )
    return back, jnp.sum(gradient * xh, axis=0, keepdims=True), jnp.sum(gradient, axis=0, keepdims=True)


def stream_flow(
    value=None,
    gain=None,
    shift=None,
    terms=None,
    above=None,
    rs=1,
    ag=1,
    keep=True,
    late=None,
    everyone=(),
    clock=(5, 30, 6, 60),
    gather_clock=(30, 6),
):
    if value is None:
        tokens, model = terms.shape[0] // rs, terms.shape[1]
    else:
        tokens, model = value.shape
    ag_bits = bits_of(ag)
    chunks = 4 if tokens % 64 == 0 else 1
    part = tokens // chunks
    flow = Flow([(TENSOR, bit) for bit in bits_of(max(rs, ag))] + list(everyone))
    if value is not None:
        value_key = flow.take(value, VMEM)
        gain_key = flow.take(gain[None], VMEM)
    if shift is not None:
        shift_key = flow.take(shift[None], VMEM)
    if above is not None:
        above_key = flow.take(above, VMEM)
        gain_sum = flow.give((1, model), F32, VMEM)
        shift_sum = flow.give((1, model), F32, VMEM)
    if rs > 1:
        terms_key = flow.take(terms)
        total_of = Sum(flow, rs, chunks, tokens, model)
    if keep:
        stream_key = flow.give((tokens, model), F32, VMEM)
    result_key = flow.give((ag * tokens, model), BF16, HBM if ag > 1 else VMEM)
    if ag > 1:
        own_key = flow.vmem(tokens, model)
        keep_sem = flow.sems(chunks)
        ag_send = flow.sems(ag, chunks)
        ag_recv = flow.sems(ag, chunks)
    if late is not None:
        late_key = flow.take(late, VMEM)
        all_key = flow.give((8, model), F32, VMEM)
        totals_key = flow.vmem(len(everyone) + 1, 8, model, dtype=F32)
        others_key = flow.vmem(len(everyone), 8, model, dtype=F32)
        totals_send = flow.sems(len(everyone))
        totals_recv = flow.sems(len(everyone))

    def rows(chunk):
        return pl.ds(chunk * part, part)

    def steps(r):
        t = lax.axis_index(TENSOR)

        def at(block, group, chunk):
            start = (peer(t, block) % group) * tokens + chunk * part
            return pl.ds(pl.multiple_of(start, 16), part)

        sent, keeps = {}, []

        def send(src, dst, block, chunk, bit):
            sent[block, chunk] = remote(
                src,
                dst,
                r[ag_send].at[block, chunk],
                r[ag_recv].at[block, chunk],
                TENSOR,
                partner(t, bit),
            )

        def finish(chunk, total):
            here = rows(chunk)
            if value is None:
                r[result_key][here, :] = total.astype(BF16)
                return
            stream = r[value_key][here, :].astype(F32)
            if above is None:
                if total is not None:
                    stream = stream + total
                    r[stream_key][here, :] = stream
                xh, unused = norm_parts(stream)
                result = (xh * r[gain_key][...] + r[shift_key][...]).astype(BF16)
            else:
                back, gains, shifts = norm_back_parts(stream, r[gain_key][...], total)
                if chunk == 0:
                    r[gain_sum][...] = gains
                    r[shift_sum][...] = shifts
                else:
                    r[gain_sum][...] += gains
                    r[shift_sum][...] += shifts
                gradient = r[above_key][here, :].astype(F32) + back
                if keep:
                    r[stream_key][here, :] = gradient
                result = gradient.astype(BF16)
            if ag == 1:
                r[result_key][here, :] = result
                return
            r[own_key][here, :] = result
            place = r[result_key].at[at(0, ag, chunk)]
            keeps.append(local_copy(r[own_key].at[here], place, r[keep_sem].at[chunk]))
            for bit in reversed(ag_bits):
                send(r[own_key].at[here], place, bit, chunk, bit)

        if rs > 1:
            yield from total_of.steps(
                r,
                lambda block, chunk: r[terms_key].at[at(block, rs, chunk)],
                rows,
                finish,
                clock,
            )
        else:
            for chunk in range(chunks):
                finish(chunk, None)
        if late is not None:
            count = late.shape[0]
            totals, others = r[totals_key], r[others_key]
            totals[0, :count] = r[late_key][...]
            totals[0, count : count + 1] = r[gain_sum][...]
            totals[0, count + 1 : count + 2] = r[shift_sum][...]
            totals[0, count + 2 :] = jnp.zeros_like(totals[0, count + 2 :])
            for i, (axis, bit) in enumerate(everyone):
                copy = remote(
                    totals.at[i],
                    others.at[i],
                    r[totals_send].at[i],
                    r[totals_recv].at[i],
                    axis,
                    partner(lax.axis_index(axis), bit),
                )
                yield clock[-1] + 40 + 15 * i
                copy.wait()
                totals[i + 1] = totals[i] + others[i]
            r[all_key][...] = totals[len(everyone)]
        first, pace = gather_clock
        for i, block in enumerate(sorted(range(2, ag, 2), key=lambda b: (level_of(b), low_bit(b)))):
            for chunk in range(chunks):
                yield first + (i * chunks + chunk) * pace
                sent[block, chunk].wait_recv()
                for bit in reversed(ag_bits):
                    if bit < low_bit(block):
                        place = r[result_key].at[at(block, ag, chunk)]
                        send(place, place, block + bit, chunk, bit)
        for (block, chunk), copy in sent.items():
            copy.wait_send()
            if block % 2:
                copy.wait_recv()
        for copy in keeps:
            copy.wait()

    flow.steps = steps
    return flow


def spread_on(side, block, bit):
    if block == 0:
        return True
    return bit < low_bit(block) if side == 0 else bit > high_bit(block)


def fetch_flow(weights, half, n_dp, window=3, clock=(8, 6.5)):
    dp_bits = bits_of(n_dp)
    units = [
        (which, plane, side)
        for which, (by_rows, weight) in enumerate(weights)
        for plane in range(weight.shape[0])
        for side in range(2)
    ]
    flow = Flow([(TENSOR, half)] + [(DP, bit) for bit in dp_bits])
    sources, targets, owns = [], [], []
    for by_rows, weight in weights:
        planes, high, wide = weight.shape
        sources.append(flow.take(weight))
        both = (planes, 2 * high, wide) if by_rows else (planes, high, 2 * wide)
        targets.append(flow.give(both, BF16))
        owns.append(flow.vmem(*weight.shape))
    sends = flow.sems(len(units), n_dp)
    recvs = flow.sems(len(units), n_dp)
    takes = flow.sems(len(weights))
    keep_sems = flow.sems(len(weights))

    def steps(r):
        t = lax.axis_index(TENSOR)
        d = lax.axis_index(DP)
        copies, keeps = {}, []

        def places(unit, block):
            which, plane, side = unit
            by_rows, weight = weights[which]
            source, target = r[sources[which]], r[targets[which]]
            high, wide = weight.shape[1:]
            size = (wide if by_rows else high) // n_dp // 2
            start = (peer(d, block) * 2 + side) * size
            if by_rows:
                columns = pl.ds(pl.multiple_of(start, 128), size)
                return source.at[plane, :, columns], target.at[plane, pl.ds(high, high), columns]
            rows = pl.ds(pl.multiple_of(start, 16), size)
            return source.at[plane, rows], target.at[plane, rows, pl.ds(wide, wide)]

        def send(src, dst, unit, block, axis, index):
            copies[unit, block] = remote(
                src, dst, r[sends].at[unit, block], r[recvs].at[unit, block], axis, index
            )

        def begin(unit):
            if unit < len(units):
                src, dst = places(units[unit], 0)
                send(src, dst, unit, 0, TENSOR, partner(t, half))

        def forward(unit, block):
            copies[unit, block].wait_recv()
            place = places(units[unit], block)[1]
            for bit in dp_bits:
                if spread_on(units[unit][2], block, bit):
                    send(place, place, unit, block + bit, DP, partner(d, bit))

        for unit in range(window):
            begin(unit)
        for which in range(len(weights)):
            keeps.append(local_copy(r[sources[which]], r[owns[which]], r[takes].at[which]))
        yield clock[0]
        for which, (by_rows, weight) in enumerate(weights):
            high, wide = weight.shape[1:]
            target = r[targets[which]]
            target = target.at[:, pl.ds(0, high)] if by_rows else target.at[:, :, pl.ds(0, wide)]
            keeps[which].wait()
            keeps[which] = local_copy(r[owns[which]], target, r[keep_sems].at[which])
        for step in range(len(units) + len(dp_bits) - 1):
            if step < len(units):
                forward(step, 0)
                begin(step + window)
            for level in range(1, len(dp_bits)):
                if 0 <= step - level < len(units):
                    for block in range(1, n_dp):
                        if level_of(block) == level:
                            forward(step - level, block)
            yield clock[0] + (step + 1) * clock[1]
        for unit in range(len(units)):
            copies[unit, n_dp - 1].wait_recv()
        for copy in copies.values():
            copy.wait_send()
        for copy in keeps:
            copy.wait()

    flow.steps = steps
    return flow


def text_flow(text, half, n, clock=(20, 12)):
    high, wide = text.shape[0] // (n // half), text.shape[1]
    flow = Flow([(TENSOR, bit) for bit in bits_of(n)])
    text_key = flow.take(text)
    result_key = flow.give((high, wide * n), BF16)
    own_key = flow.vmem(high, wide)
    sends, recvs, keeps = flow.sems(n), flow.sems(n), flow.sems(2)

    def steps(r):
        t = lax.axis_index(TENSOR)
        row = t // half
        copies = {}

        def rows(which):
            return r[text_key].at[pl.ds(pl.multiple_of(which * high, 16), high)]

        def columns(block):
            return r[result_key].at[:, pl.ds(pl.multiple_of(peer(t, block) * wide, 128), wide)]

        def send(src, dst, block, bit):
            copies[block] = remote(
                src, dst, r[sends].at[block], r[recvs].at[block], TENSOR, partner(t, bit)
            )

        for bit in reversed(bits_of(n)):
            send(rows(1 - row if bit == half else row), columns(0), bit, bit)
        keep = local_copy(rows(row), r[own_key], r[keeps].at[0])
        yield clock[0]
        keep.wait()
        keep = local_copy(r[own_key], columns(0), r[keeps].at[1])
        for i, block in enumerate(sorted(range(1, n), key=lambda b: (level_of(b), low_bit(b)))):
            copies[block].wait_recv()
            for bit in reversed(bits_of(n)):
                if bit < low_bit(block):
                    send(columns(block), columns(block), block + bit, bit)
            yield clock[0] + i * clock[1]
        for copy in copies.values():
            copy.wait_send()
        keep.wait()

    flow.steps = steps
    return flow


def text_back_flow(terms, half, n, clocks=((8, 30, 6, 30), (9, 30, 6, 35), 45)):
    high, wide = terms.shape[0], terms.shape[1] // n
    flow = Flow([(TENSOR, bit) for bit in bits_of(n)])
    terms_key = flow.take(terms)
    result_key = flow.give((high * (n // half), wide), BF16)
    sums = [Sum(flow, half, 1, high, wide) for unused in range(2)]
    owns = [flow.vmem(high, wide) for unused in range(2)]
    sems = flow.sems(3)

    def steps(r):
        t = lax.axis_index(TENSOR)
        row = t // half
        last = []

        def view(far):
            def place(block, chunk):
                column = peer(t, block + far) * wide
                return r[terms_key].at[:, pl.ds(pl.multiple_of(column, 128), wide)]

            return place

        def target():
            return r[result_key].at[pl.ds(pl.multiple_of(row * high, 16), high)]

        def finish_far(chunk, total):
            r[owns[0]][...] = total.astype(BF16)
            last.append(
                remote(
                    r[owns[0]],
                    target(),
                    r[sems].at[0],
                    r[sems].at[1],
                    TENSOR,
                    partner(t, half),
                )
            )

        def finish_near(chunk, total):
            r[owns[1]][...] = total.astype(BF16)
            last.append(local_copy(r[owns[1]], target(), r[sems].at[2]))

        def rows(chunk):
            return pl.ds(0, high)

        parts = [
            [0, sums[0].steps(r, view(half), rows, finish_far, clocks[0])],
            [0, sums[1].steps(r, view(0), rows, finish_near, clocks[1])],
        ]
        while parts:
            entry = min(parts, key=lambda e: e[0])
            if entry[0]:
                yield entry[0]
            moment = next(entry[1], None)
            if moment is None:
                parts.remove(entry)
            else:
                entry[0] = moment
        yield clocks[2]
        for copy in last:
            copy.wait()

    flow.steps = steps
    return flow


def grads_flow(grads, n_dp, outs, half=0, summing=True, window=4, clock=(10, 20), slack=1):
    high, whole = grads[0].shape[1:]
    high = high if summing else high * n_dp
    wide = whole // 2 if half else whole
    size = high // n_dp // 2
    dp_bits = bits_of(n_dp)
    units = [
        (which, plane, side)
        for which, grad in enumerate(grads)
        for plane in range(grad.shape[0])
        for side in range(2)
    ]
    count = len(units)
    depth = len(dp_bits)
    slots = n_dp // 2 if summing else 1
    flow = Flow([(DP, bit) for bit in dp_bits] + ([(TENSOR, half)] if half else []))
    sources = [flow.take(grad) for grad in grads]
    targets = [flow.give((n, high, wide) if n else (wide, high), BF16) for n in outs]
    target_of = [(i, plane) for i, n in enumerate(outs) for plane in range(max(n, 1))]
    flat = [(grad, plane) for grad in range(len(grads)) for plane in range(grads[grad].shape[0])]
    gathered = flow.vmem(len(flat), high, wide)
    turned = [unit for unit in range(count) if not outs[target_of[flat.index(units[unit][:2])][0]]]
    if turned:
        staged = flow.vmem(len(turned), n_dp, wide, size)
    if summing:
        held = flow.vmem(count, slots, size, whole)
    load_sems = flow.sems(count, slots)
    if summing:
        came = flow.vmem(count, n_dp - 1, size, whole)
        sum_send, sum_recv = flow.sems(count, n_dp), flow.sems(count, n_dp)
    if half:
        given = flow.vmem(count, size, wide)
        mid_send, mid_recv = flow.sems(count), flow.sems(count)
        if summing:
            mine = flow.vmem(count, size, wide, dtype=F32)
            theirs = flow.vmem(count, size, wide)
    ag_send, ag_recv = flow.sems(count, n_dp), flow.sems(count, n_dp)
    keep_sems = flow.sems(count, n_dp)

    def order(side):
        return dp_bits if side == 0 else tuple(reversed(dp_bits))

    def stage(side, block):
        return min(i for i, bit in enumerate(order(side)) if block & bit)

    def slot(side, block):
        return [b for b in range(n_dp) if b == 0 or stage(side, b) > 0].index(block)

    def steps(r):
        d = lax.axis_index(DP)
        sums, loads, mids, spreads, keeps = {}, {}, {}, {}, []

        def rows_of(unit, block):
            return pl.ds(pl.multiple_of((peer(d, block) * 2 + units[unit][2]) * size, 16), size)

        def source_of(unit, block):
            which, plane, side = units[unit]
            rows = rows_of(unit, block) if summing else pl.ds(side * size, size)
            return r[sources[which]].at[plane, rows]

        def region(unit, block):
            return r[gathered].at[flat.index(units[unit][:2]), rows_of(unit, block)]

        def swap(src, unit):
            mids[unit] = remote(
                src,
                r[given].at[unit],
                r[mid_send].at[unit],
                r[mid_recv].at[unit],
                TENSOR,
                partner(lax.axis_index(TENSOR), half),
            )

        def send(src, unit, block):
            side = units[unit][2]
            sums[unit, block] = remote(
                src,
                r[came].at[unit, block - 1],
                r[sum_send].at[unit, block],
                r[sum_recv].at[unit, block],
                DP,
                partner(d, order(side)[stage(side, block)]),
            )

        def summed(unit, block):
            side = units[unit][2]
            loads[unit, block].wait()
            total = r[held][unit, slot(side, block)].astype(F32)
            for i, bit in enumerate(order(side)):
                if summing and (block == 0 or i < stage(side, block)):
                    sums[unit, block + bit].wait_recv()
                    total = total + r[came][unit, block + bit - 1].astype(F32)
            return total

        def begin(unit):
            if unit >= count:
                return
            side = units[unit][2]
            if not summing:
                source = source_of(unit, 0)
                swap(source.at[:, pl.ds(wide, wide)], unit)
                loads[unit, 0] = local_copy(
                    source.at[:, pl.ds(0, wide)], region(unit, 0), r[load_sems].at[unit, 0]
                )
                return
            for block in range(n_dp):
                source = source_of(unit, block)
                if block and stage(side, block) == 0:
                    send(source, unit, block)
                else:
                    place = slot(side, block)
                    loads[unit, block] = local_copy(
                        source, r[held].at[unit, place], r[load_sems].at[unit, place]
                    )

        def middle(unit, level):
            side = units[unit][2]
            for block in range(1, n_dp):
                if stage(side, block) == level:
                    r[held][unit, slot(side, block)] = summed(unit, block).astype(BF16)
                    send(r[held].at[unit, slot(side, block)], unit, block)

        def cross(unit):
            if half and summing:
                total = summed(unit, 0)
                r[mine][unit] = total[:, :wide]
                r[theirs][unit] = total[:, wide:].astype(BF16)
                swap(r[theirs].at[unit], unit)

        def spread(unit, block, src, dst):
            for bit in dp_bits:
                if spread_on(units[unit][2], block, bit):
                    spreads[unit, block + bit] = remote(
                        src,
                        dst,
                        r[ag_send].at[unit, block + bit],
                        r[ag_recv].at[unit, block + bit],
                        DP,
                        partner(d, bit),
                    )

        def settle(unit):
            place = region(unit, 0)
            if half and summing:
                total = r[mine][unit]
            elif summing:
                total = summed(unit, 0)
            else:
                loads[unit, 0].wait()
                total = place[...].astype(F32)
            if half:
                mids[unit].wait_recv()
                total = total + r[given][unit].astype(F32)
            place[...] = total.astype(BF16)
            spread(unit, 0, place, place)

        def onward(unit, level):
            for block in range(1, n_dp):
                if level_of(block) == level:
                    spreads[unit, block].wait_recv()
                    place = region(unit, block)
                    spread(unit, block, place, place)

        def write(unit):
            spreads[unit, n_dp - 1].wait_recv()
            which, plane = target_of[flat.index(units[unit][:2])]
            target = r[targets[which]]
            for block in range(n_dp):
                src = region(unit, block)
                if outs[which]:
                    to = target.at[plane, rows_of(unit, block)]
                else:
                    place = turned.index(unit)
                    r[staged][place, block] = src[...].astype(F32).T.astype(BF16)
                    src = r[staged].at[place, block]
                    start = (peer(d, block) * 2 + units[unit][2]) * size
                    to = target.at[:, pl.ds(pl.multiple_of(start, 128), size)]
                keeps.append(local_copy(src, to, r[keep_sems].at[unit, block]))

        for unit in range(window):
            begin(unit)
        start = max(depth - 1, 0) if summing else 0
        first = start + (1 if summing else 0) + (slack if half else 0)
        for step in range(count + first + depth):
            yield clock[0] + step * clock[1]

            def turn(lag, action, *more):
                if 0 <= step - lag < count:
                    action(step - lag, *more)

            turn(first + depth, write)

            for level in range(depth - 1, 0, -1):
                turn(first + level, onward, level)
            turn(first, settle)
            turn(start, cross)
            if summing:
                for level in range(depth - 1, 0, -1):
                    turn(level - 1, middle, level)
            begin(step + window)
        for copy in [*sums.values(), *mids.values(), *spreads.values()]:
            copy.wait_send()
        for copy in keeps:
            copy.wait()

    flow.steps = steps
    return flow


def dot_flow(left, right, turned=False, parts=8, clock=(4, 8)):
    flow = Flow([])
    high, deep = left.shape
    wide = right.shape[0] if turned else right.shape[1]
    part = high // parts
    left_key, right_key = flow.take(left), flow.take(right)
    result_key = flow.give((high, wide), BF16)
    lefts, rights = flow.vmem(2, part, deep), flow.vmem(*right.shape)
    results = flow.vmem(2, part, wide)
    sems, right_sem = flow.sems(2, 2), flow.sems(1)

    def steps(r):
        loads, stores = {}, {}

        def load(i):
            if i < parts:
                loads[i] = local_copy(
                    r[left_key].at[pl.ds(i * part, part)], r[lefts].at[i % 2], r[sems].at[0, i % 2]
                )

        whole = local_copy(r[right_key], r[rights], r[right_sem].at[0])
        load(0)
        load(1)
        for i in range(parts):
            yield clock[0] + i * clock[1]
            if i == 0:
                whole.wait()
            loads[i].wait()
            if i > 1:
                stores[i - 2].wait()
            dims = (((1,), (1 if turned else 0,)), ((), ()))
            value = lax.dot_general(
                r[lefts][i % 2], r[rights][...], dims, preferred_element_type=F32
            )
            r[results][i % 2] = value.astype(BF16)
            stores[i] = local_copy(
                r[results].at[i % 2], r[result_key].at[pl.ds(i * part, part)], r[sems].at[1, i % 2]
            )
            load(i + 2)
        for i in range(max(parts - 2, 0), parts):
            stores[i].wait()

    flow.steps = steps
    return flow


def pass_flow(value):
    flow = Flow([])
    value_key = flow.take(value)
    result_key = flow.give(value.shape, value.dtype)
    held = flow.vmem(*value.shape)
    sems = flow.sems(2)

    def steps(r):
        copy = local_copy(r[value_key], r[held], r[sems].at[0])
        yield 8
        copy.wait()
        copy = local_copy(r[held], r[result_key], r[sems].at[1])
        yield 30
        copy.wait()

    flow.steps = steps
    return flow


def nothing(*refs):
    pass


def after(value, *before):
    return pl.pallas_call(
        nothing,
        in_specs=[HBM] * (1 + len(before)),
        out_specs=HBM,
        out_shape=jax.ShapeDtypeStruct(value.shape, value.dtype),
        input_output_aliases={0: 0},
    )(value, *before)


def local(
    image,
    text,
    cotangent,
    norm_gains,
    norm_shifts,
    w_self,
    w_self_out,
    w_cross_q,
    w_cross_kv,
    w_cross_out,
    w_text,
    w_up,
    w_down,
    segment_ids,
    caption_lengths,
):
    rows_here = segment_ids.shape[0]
    n_tensor = lax.axis_size(TENSOR)
    n_dp = lax.axis_size(DP)
    half = n_tensor // rows_here
    row = lax.axis_index(TENSOR) // half
    width = w_self.shape[2]
    slots = IMGS * CAP

    seg = lax.dynamic_index_in_dim(segment_ids, row, 0, keepdims=False)
    seg_col = seg[:, None]
    seg_row = seg[None, :]
    lengths = lax.dynamic_index_in_dim(caption_lengths.reshape(rows_here, IMGS), row, 0, keepdims=False)
    slot = jnp.arange(slots, dtype=jnp.int32)
    live = (slot % CAP) < jnp.repeat(lengths, CAP)
    slot_row = jnp.where(live, slot // CAP, -1)[None, :]

    (w_self2, w_self_out2), (n1,), (later,), (text_columns,) = run_flows(
        0,
        "start",
        60,
        fetch_flow(((False, w_self), (True, w_self_out[None])), half, n_dp),
        stream_flow(
            image, norm_gains[0], norm_shifts[0], ag=half, keep=False, gather_clock=(12, 11)
        ),
        pass_flow(cotangent),
        dot_flow(text, w_text),
    )
    w_self_out2 = w_self_out2[0]
    triple = planes_of(n1, w_self2)
    o1 = attend(seg_col, seg_row, (triple, 0), (triple, 1), (triple, 2))
    p1 = dot(o1, w_self_out2).astype(BF16)
    e3 = lax.all_gather(later, TENSOR, axis=0, tiled=True)
    (x1, n2), (w_kv2, w_cross_q2, w_cross_out2), (projected,) = run_flows(
        1,
        "self_sum",
        100,
        stream_flow(
            image,
            norm_gains[1],
            norm_shifts[1],
            terms=p1,
            rs=half,
            ag=half,
            clock=(5, 0, 10, 18),
            gather_clock=(60, 10),
        ),
        fetch_flow(
            ((False, w_cross_kv), (False, w_cross_q[None]), (True, w_cross_out[None])),
            half,
            n_dp,
            clock=(20, 8),
        ),
        text_flow(text_columns, half, n_tensor),
    )
    w_cross_q2, w_cross_out2 = w_cross_q2[0], w_cross_out2[0]

    pair = planes_of(projected, w_kv2)
    q2 = dot(n2, w_cross_q2).astype(BF16)
    o2 = attend(seg_col, slot_row, (q2, None), (pair, 0), (pair, 1))
    p2 = dot(o2, w_cross_out2).astype(BF16)
    (x2, n3), (active_back,) = run_flows(
        2,
        "cross_sum",
        100,
        stream_flow(
            x1,
            norm_gains[2],
            norm_shifts[2],
            terms=p2,
            rs=half,
            ag=n_tensor,
            clock=(5, 0, 6, 15),
            gather_clock=(40, 6),
        ),
        dot_flow(e3, w_down, True, clock=(4, 11)),
    )

    act, dh = hidden_step(n3, w_up, active_back)
    down_grad = dot_t(act, e3).astype(BF16)
    up_grad = dot_t(n3, dh).astype(BF16)
    sums = lax.psum((down_grad, up_grad), DP)
    p3 = after(rows_dot([dh], w_up[None]), down_grad, up_grad)
    (gain_two, shift_two, g2, e2), (p6,) = run_flows(
        3,
        "up_sum",
        100,
        stream_flow(
            x2, norm_gains[2], terms=p3, above=cotangent, rs=n_tensor, ag=half, clock=(8, 30, 6, 60)
        ),
        dot_flow(act, w_down, clock=(12, 10)),
    )

    do2 = dot_r(e2, w_cross_out2).astype(BF16)
    dq2, dk2, dv2 = attend_back(seg_col, slot_row, (q2, None), (pair, 0), (pair, 1), do2)
    p4 = rows_dot([dq2], w_cross_q2[None])
    pair_back = jnp.stack([dk2, dv2])
    cross = jnp.concatenate(
        [
            dot_t(n2, dq2).astype(BF16)[None],
            planes_grad(projected, pair_back),
            dot_t(e2, o2).astype(BF16)[None],
        ]
    )
    cross_part = lax.psum_scatter(cross, DP, scatter_dimension=1, tiled=True)
    dproj = rows_dot([dk2, dv2], w_kv2)
    (gain_one, shift_one, g1, e1), (dproj,) = run_flows(
        4,
        "query_sum",
        60,
        stream_flow(
            x1,
            norm_gains[1],
            terms=after(p4, cross),
            above=g2,
            rs=half,
            ag=half,
            clock=(5, 0, 6, 15),
            gather_clock=(37, 6),
        ),
        text_back_flow(dproj, half, n_tensor),
    )

    down_sum = lax.psum_scatter(after(p6, e1), TENSOR, scatter_dimension=0, tiled=True)
    image_out = (x2 + down_sum.astype(F32)).astype(BF16)

    do1 = dot_r(e1, w_self_out2).astype(BF16)
    dq1, dk1, dv1 = attend_back(seg_col, seg_row, (triple, 0), (triple, 1), (triple, 2), do1)
    triple_back = jnp.stack([dq1, dk1, dv1])
    own = planes_grad(n1, triple_back)
    own_out = dot_t(e1, o1).astype(BF16)[None]
    p5 = planes_back(triple_back, w_self2)
    text_w_part = columns_dot(text, dproj)
    p7, p8 = [rows_dot([dproj], part[None], 1024) for part in jnp.split(w_text, 2)]
    text_right = lax.psum_scatter(p8, TENSOR, scatter_dimension=0, tiled=True)
    everyone = [(TENSOR, bit) for bit in bits_of(n_tensor)] + [(DP, bit) for bit in bits_of(n_dp)]
    late = jnp.concatenate([gain_one, shift_one, gain_two, shift_two])
    (
        (self_grad, self_out_grad),
        (unused, unused, image_grad, all_sums),
        (text_left,),
        (cross_q_grad, cross_kv_grad, cross_out_grad),
        (text_w_grad,),
    ) = run_flows(
        5,
        "end",
        200,
        grads_flow((own, own_out), n_dp, (3, 0), half, clock=(14, 14)),
        stream_flow(
            image,
            norm_gains[0],
            terms=p5,
            above=g1,
            rs=half,
            keep=False,
            late=late,
            everyone=everyone,
            clock=(6, 0, 8, 50),
        ),
        stream_flow(terms=p7, rs=n_tensor, keep=False, clock=(7, 45, 11, 110)),
        grads_flow((cross_part,), n_dp, (1, 2, 0), half, summing=False, clock=(15, 12)),
        grads_flow((text_w_part.reshape(4, -1, width),), n_dp, (4,), clock=(10, 16)),
    )
    down_grad, up_grad = [value.astype(F32) for value in sums]
    self_grad, self_out_grad = self_grad.astype(F32), self_out_grad.astype(F32)
    text_grad = jnp.concatenate([text_left, text_right], axis=1)
    cross_q_grad, cross_kv_grad = cross_q_grad[0].astype(F32), cross_kv_grad.astype(F32)
    cross_out_grad = cross_out_grad.astype(F32)
    text_w_grad = text_w_grad.reshape(-1, width).astype(F32)
    gain_grad = jnp.stack([all_sums[4], all_sums[0], all_sums[2]])
    shift_grad = jnp.stack([all_sums[5], all_sums[1], all_sums[3]])
    return (
        image_out,
        image_grad,
        text_grad,
        gain_grad,
        shift_grad,
        self_grad,
        self_out_grad,
        cross_q_grad,
        cross_kv_grad,
        cross_out_grad,
        text_w_grad,
        up_grad,
        down_grad,
    )


def solution(mesh):
    tokens = P((DP, TENSOR), None)
    columns = P(None, TENSOR)
    planes = P(None, None, TENSOR)
    rows = P(TENSOR, None)
    return jax.shard_map(
        local,
        mesh=mesh,
        in_specs=(
            tokens,
            P(DP, None),
            tokens,
            P(),
            P(),
            planes,
            rows,
            columns,
            planes,
            rows,
            columns,
            columns,
            rows,
            P(DP, None),
            P(DP),
        ),
        out_specs=(
            tokens,
            tokens,
            tokens,
            P(),
            P(),
            planes,
            rows,
            columns,
            planes,
            rows,
            columns,
            columns,
            rows,
        ),
        check_vma=False,
    )
```
